32 devices in a mesh: gx: 8 (over y, x, core), gy: 4 (over z).
Axes of the slice: x: 2, y: 2, z: 4, core: 2. Of those that a mesh axis runs over, the one named last changes fastest.
Arguments:
- labels: float32 [32768, 512], P(('gx', 'gy')), may hold values from -6 to 6
- point_order: int32 [32, 1024], P(('gx', 'gy')), may hold values from 0 to 1023, each once within a row
- leaf_inverse: float32 [32768, 1024], P(('gx', 'gy')), as said below
- leaf_basis: float32 [32768, 256], P(('gx', 'gy')), may hold values from -0.1875 to 0.1875
- couple_one: float32 [8192, 1024], P(('gx', 'gy'))
- transfer_one: float32 [8192, 256], P(('gx', 'gy')), may hold values from -0.1875 to 0.1875
- couple_two: float32 [2048, 1024], P(('gx', 'gy'))
- transfer_two: float32 [2048, 256], P(('gx', 'gy')), may hold values from -0.1875 to 0.1875
- couple_top: float32 [1024, 256], P(('gx', 'gy'))
Outputs:
- solution: float32 [32768, 512], P(('gx', 'gy'))
The draws below stay inside these ranges and needn't reach their ends.
Inputs may be any that keep to these rules, and one draw needn't show every extreme that they name: Each row of point_order is a permutation of 0 to 1023. leaf_inverse, couple_one, couple_two and the top matrix assembled from couple_top are dense with a dominant diagonal.
All inputs are finite; a program needn't handle non-finite values.
Results may differ from the reference program's by a relative error of at most 0.00011.
Values sent between devices are 32-bit elements; how exact they have to be, the bound alone decides.
A program may use at most 64 MiB of HBM per device.

```python
import math
import jax
import jax.numpy as jnp
from jax import lax

LEAF = 1024
RANK = 256
COLS = 512
NLEAF = 32
NTOP = 2
POINTS = 32768


def dominant(key, height, breadth):
    key_diag, key_rest = jax.random.split(jax.random.fold_in(key, 7))
    diagonal = jnp.exp(jax.random.uniform(key_diag, (height, 1), jnp.float32, math.log(0.5), math.log(2.0)))
    spread_part = jax.random.normal(key_rest, (height, breadth), jnp.float32) * (0.5 / math.sqrt(breadth))
    row_pos = lax.broadcasted_iota(jnp.int32, (height, breadth), 0) % breadth
    col_pos = lax.broadcasted_iota(jnp.int32, (height, breadth), 1)
    return spread_part + jnp.where(row_pos == col_pos, diagonal, 0.0)


def draw_leaf_inverse(key, part):
    return dominant(key, NLEAF * LEAF, LEAF)


def draw_couple_one(key, part):
    return dominant(key, NLEAF * RANK, 4 * RANK)


def draw_couple_two(key, part):
    return dominant(key, NLEAF * RANK // 4, 4 * RANK)


def draw_couple_top(key, part):
    full_top = dominant(key, NTOP * RANK, NTOP * RANK)
    slice_rows = RANK // 16
    return full_top.reshape(NTOP, 16, slice_rows, NTOP, RANK).transpose(3, 1, 0, 2, 4).reshape(NTOP * NTOP * RANK, RANK)


def shard_levels(stream_key, dims, shards, low, top_value):
    def one(position, shards_of):
        heights = jax.random.uniform(jax.random.fold_in(jax.random.fold_in(stream_key, 6), position), (shards_of,), jnp.float32, low / len(shards), top_value / len(shards))
        return jnp.repeat(jnp.exp(heights), dims[position] // shards_of).reshape((-1,) + (1,) * (len(dims) - position - 1))

    gain = one(*shards[0])
    for cut in shards[1:]:
        gain = gain * one(*cut)
    return gain


def noise(stream_key, dims, deviation, most, cuts=(), dtype=jnp.bfloat16):
    drawn = deviation * jax.random.normal(stream_key, dims, jnp.float32)
    if cuts:
        drawn = drawn * shard_levels(stream_key, dims, cuts, -0.22, 0.18)
    return jnp.clip(drawn, -most, most).astype(dtype)


def setup_inputs(seed: int = 0) -> dict:
    key_list = jax.random.split(jax.random.key(seed), 10)
    labels = noise(key_list[0], (POINTS, COLS), 1.0, 6.0, ((0, 32),), jnp.float32)
    point_order = jax.vmap(lambda own: jax.random.permutation(own, LEAF))(jax.random.split(key_list[1], NLEAF)).reshape((NLEAF, LEAF)).astype(jnp.int32)
    leaf_inverse = draw_leaf_inverse(jax.random.fold_in(key_list[9], 71), 0)
    leaf_basis = noise(key_list[3], (POINTS, RANK), LEAF ** -0.5, 0.1875, ((0, 32),), jnp.float32)
    couple_one = draw_couple_one(jax.random.fold_in(key_list[9], 71), 0)
    transfer_one = noise(key_list[5], (NLEAF * RANK, RANK), (4 * RANK) ** -0.5, 0.1875, ((0, 32),), jnp.float32)
    couple_two = draw_couple_two(jax.random.fold_in(key_list[9], 71), 0)
    transfer_two = noise(key_list[7], (NLEAF * RANK // 4, RANK), (4 * RANK) ** -0.5, 0.1875, ((0, 32),), jnp.float32)
    couple_top = draw_couple_top(jax.random.fold_in(key_list[9], 71), 0)
    return {"labels": labels, "point_order": point_order, "leaf_inverse": leaf_inverse, "leaf_basis": leaf_basis, "couple_one": couple_one, "transfer_one": transfer_one, "couple_two": couple_two, "transfer_two": transfer_two, "couple_top": couple_top}


def batched(left, right):
    return jnp.einsum("nij,njc->nic", left, right, precision=lax.Precision.HIGHEST)


def batched_left(left, right):
    return jnp.einsum("nir,nic->nrc", left, right, precision=lax.Precision.HIGHEST)


def reference(labels, point_order, leaf_inverse, leaf_basis, couple_one, transfer_one, couple_two, transfer_two, couple_top):
    nodes_one = NLEAF // 4
    nodes_two = NLEAF // 16
    slice_rows = RANK // 16
    blocks = labels.reshape(NLEAF, LEAF, COLS)
    rhs = jax.vmap(lambda block, index: block[index])(blocks, point_order)
    inverse = leaf_inverse.reshape(NLEAF, LEAF, LEAF)
    basis = leaf_basis.reshape(NLEAF, LEAF, RANK)
    solved = batched(inverse, rhs)
    proj = batched_left(basis, solved)
    couple_a = couple_one.reshape(nodes_one, 4 * RANK, 4 * RANK)
    trans_a = transfer_one.reshape(nodes_one, 4 * RANK, RANK)
    solve_one = batched(couple_a, proj.reshape(nodes_one, 4 * RANK, COLS))
    reduced_one = batched_left(trans_a, solve_one)
    couple_b = couple_two.reshape(nodes_two, 4 * RANK, 4 * RANK)
    trans_b = transfer_two.reshape(nodes_two, 4 * RANK, RANK)
    solve_two = batched(couple_b, reduced_one.reshape(nodes_two, 4 * RANK, COLS))
    reduced_two = batched_left(trans_b, solve_two)
    full_top = couple_top.reshape(NTOP, 16, NTOP, slice_rows, RANK).transpose(2, 1, 3, 0, 4).reshape(NTOP * RANK, NTOP * RANK)
    solve_top = jnp.dot(full_top, reduced_two.reshape(NTOP * RANK, COLS), precision=lax.Precision.HIGHEST)
    block_two = solve_top.reshape(nodes_two, RANK, COLS)
    fixed_two = solve_two - batched(couple_b, batched(trans_b, block_two))
    block_one = fixed_two.reshape(nodes_one, RANK, COLS)
    fixed_one = solve_one - batched(couple_a, batched(trans_a, block_one))
    block_leaf = fixed_one.reshape(NLEAF, RANK, COLS)
    tree = solved - batched(inverse, batched(basis, block_leaf))
    placed = jax.vmap(lambda block, index: jnp.zeros_like(block).at[index].set(block))(tree, point_order)
    return placed.reshape(NLEAF * LEAF, COLS)
```

```python
import functools

import jax
import jax.numpy as jnp
from jax import lax
from jax.experimental import pallas as pl
from jax.experimental.pallas import tpu as pltpu
from jax.sharding import PartitionSpec as P

F32 = jnp.float32
BF16 = jnp.bfloat16
FAN = 4


def split(x):
    high = x.astype(BF16)
    return high, (x - high.astype(F32)).astype(BF16)


def dot(left, right):
    return jnp.dot(left, right, preferred_element_type=F32)


def dot3(left, right):
    return dot(left[0], right[0]) + (dot(left[0], right[1]) + dot(left[1], right[0]))


def matmul(left, right):
    return dot3(split(left), split(right))


def flat(block):
    return block.reshape(-1, block.shape[-1])


def kernel(
    depth,
    groups,
    tile,
    labels,
    order,
    inverse,
    basis,
    couple_one,
    transfer_one,
    couple_two,
    transfer_two,
    couple_top,
    placed_out,
    spread_out,
    block_out,
    lab_high,
    lab_low,
    sol_high,
    sol_low,
    column,
    proj_all,
    trans_one_all,
    couple_two_all,
    fixed_two_all,
    reduce_part,
    reduce_in,
    stack_two,
    trans_two_all,
    top_part,
    top_in,
    top_all,
    block_two,
    top_rows,
    solve_one,
    gain_one,
    line_send,
    line_recv,
    row_send,
    row_recv,
    quad_send,
    quad_recv,
    wide_send,
    wide_recv,
    tops_send,
    tops_recv,
):
    index = lax.axis_index("gx") * depth + lax.axis_index("gy")
    r = index % FAN
    sid = index // FAN
    q = sid % FAN
    g = sid // FAN
    wide = FAN * groups
    leaf, cols = labels.shape
    rank = basis.shape[1]
    part_cols = cols // FAN
    part_rows = rank // FAN
    slice_rows = couple_top.shape[0] // groups

    def device(sid_of, r_of):
        place = sid_of * FAN + r_of
        return (place // depth, place % depth)

    def copy(source, target, send, recv, where):
        return pltpu.make_async_remote_copy(
            src_ref=source,
            dst_ref=target,
            send_sem=send,
            recv_sem=recv,
            device_id=where,
            device_id_type=pl.DeviceIdType.MESH,
        )

    def line_copy(buf, which, way, step):
        slot = r - step if way == 0 else r + step
        to = r + 1 if way == 0 else r - 1
        slot = jnp.clip(slot, 0, FAN - 1)
        to = jnp.clip(to, 0, FAN - 1)
        return copy(
            buf.at[slot],
            buf.at[slot],
            line_send.at[which, way, step],
            line_recv.at[which, way, step],
            device(sid, to),
        )

    def sends(way, step):
        if way == 0:
            return jnp.logical_and(r >= step, r < FAN - 1)
        return jnp.logical_and(r + step <= FAN - 1, r > 0)

    def receives(way, step):
        if way == 0:
            return r - 1 - step >= 0
        return r + 1 + step <= FAN - 1

    def line_start(buf, which, step):
        for way in range(2):
            @pl.when(sends(way, step))
            def _():
                line_copy(buf, which, way, step).start()

    def line_wait(buf, which, step):
        for way in range(2):
            @pl.when(receives(way, step))
            def _():
                slot = r - 1 - step if way == 0 else r + 1 + step
                slot = jnp.clip(slot, 0, FAN - 1)
                copy(
                    buf.at[slot],
                    buf.at[slot],
                    line_send.at[which, way, step],
                    line_recv.at[which, way, step],
                    device(sid, (r + 1) % FAN),
                ).wait_recv()

    def line_finish(buf, which):
        for step in range(FAN - 1):
            for way in range(2):
                @pl.when(sends(way, step))
                def _():
                    line_copy(buf, which, way, step).wait_send()

    def over_row(which, source, target, step):
        return copy(
            source, target, row_send.at[which, step - 1], row_recv.at[which, step - 1],
            device(sid, (r + step) % FAN),
        )

    def over_quad(which, source, target, step):
        return copy(
            source, target, quad_send.at[which, step - 1], quad_recv.at[which, step - 1],
            device(g * FAN + (q + step) % FAN, r),
        )

    def over_wide(source, target, step):
        return copy(
            source, target, wide_send.at[step - 1], wide_recv.at[step - 1],
            device((sid + step) % wide, r),
        )

    def over_tops(source, target, step):
        return copy(
            source, target, tops_send.at[step - 1], tops_recv.at[step - 1],
            device((g + step) % groups * FAN + q, r),
        )

    barrier = pltpu.get_barrier_semaphore()
    for step in range(1, FAN):
        pl.semaphore_signal(
            barrier, inc=1, device_id=device(sid, (r + step) % FAN),
            device_id_type=pl.DeviceIdType.MESH,
        )
    for step in range(1, wide):
        pl.semaphore_signal(
            barrier, inc=1, device_id=device((sid + step) % wide, r),
            device_id_type=pl.DeviceIdType.MESH,
        )
    pl.semaphore_wait(barrier, FAN - 1 + wide - 1)

    couple_two_all[r] = couple_two[...]
    trans_one_all[r] = transfer_one[...]
    trans_two_all[q, r] = transfer_two[...]
    top_rows[r, g] = couple_top[pl.ds(pl.multiple_of(g * slice_rows, slice_rows), slice_rows), :]
    line_start(couple_two_all, 1, 0)
    row_two = [
        over_row(0, trans_two_all.at[q, r], trans_two_all.at[q, r], s) for s in range(1, FAN)
    ]
    for c in row_two:
        c.start()
    tops = []
    for s in range(1, groups):
        other = (g + s) % groups
        tops.append(
            over_tops(
                couple_top.at[pl.ds(pl.multiple_of(other * slice_rows, slice_rows), slice_rows)],
                top_rows.at[r, g],
                s,
            )
        )
        tops[-1].start()

    lab_high[...], lab_low[...] = split(labels[...])
    position = jnp.broadcast_to(order[...].astype(F32), (128, leaf)).T
    column[...] = position.astype(jnp.int32)
    rhs_high, rhs_low = placed_high, placed_low = sol_high.at[0], sol_low.at[0]
    sol_h, sol_l = sol_high.at[1], sol_low.at[1]
    tiles = leaf // tile

    def rows_of(step):
        return pl.ds(pl.multiple_of(step * tile, tile), tile)

    @pl.loop(0, tiles)
    def _(step):
        rows = rows_of(step)
        hot = column[rows, 0:1] == lax.broadcasted_iota(jnp.int32, (tile, leaf), 1)
        hot = hot.astype(F32).astype(BF16)
        rhs_high[rows, :] = dot(hot, lab_high[...]).astype(BF16)
        rhs_low[rows, :] = dot(hot, lab_low[...]).astype(BF16)

    @pl.loop(0, tiles)
    def _(step):
        rows = rows_of(step)
        value = dot3(split(inverse[rows, :]), (rhs_high[...], rhs_low[...]))
        sol_h[rows, :], sol_l[rows, :] = split(value)

    proj_all[r] = dot3(split(basis[...].T), (sol_h[...], sol_l[...]))
    line_start(proj_all, 0, 0)

    basis_parts = split(basis[...])
    lab_high[:, :rank], lab_low[:, :rank] = basis_parts

    @pl.loop(0, tiles)
    def _(step):
        rows = rows_of(step)
        value = dot3(split(inverse[rows, :]), (lab_high[:, :rank], lab_low[:, :rank]))
        rhs_high[rows, :rank], rhs_low[rows, :rank] = split(value)

    line_wait(proj_all, 0, 0)
    line_start(proj_all, 0, 1)

    @pl.loop(0, tiles)
    def _(step):
        rows = rows_of(step)
        hot = (lax.broadcasted_iota(jnp.int32, (tile, leaf), 0) + step * tile) == order[...]
        hot = hot.astype(F32).astype(BF16)
        placed_out[rows, :] = dot(hot, sol_h[...]) + dot(hot, sol_l[...])
        spread_out[rows, :] = dot(hot, rhs_high[:, :rank]) + dot(hot, rhs_low[:, :rank])

    for c in row_two:
        c.wait_recv()
    for c in tops:
        c.wait_recv()
    quad_two = [
        over_quad(0, trans_two_all.at[q], trans_two_all.at[q], s) for s in range(1, FAN)
    ]
    row_top = [over_row(1, top_rows.at[r], top_rows.at[r], s) for s in range(1, FAN)]
    for c in quad_two + row_top:
        c.start()

    line_wait(proj_all, 0, 1)
    line_start(proj_all, 0, 2)
    line_wait(couple_two_all, 1, 0)
    line_start(couple_two_all, 1, 1)
    line_wait(proj_all, 0, 2)

    solve_one[...] = matmul(couple_one[...], flat(proj_all[...]))
    reduced = matmul(transfer_one[...].T, solve_one[...])
    for part in range(FAN):
        reduce_part[part] = reduced[:, part * part_cols : (part + 1) * part_cols]
    row_reduce = [
        over_row(2, reduce_part.at[(r + s) % FAN], reduce_in.at[s - 1], s) for s in range(1, FAN)
    ]
    for c in row_reduce:
        c.start()
    line_wait(couple_two_all, 1, 1)
    line_start(couple_two_all, 1, 2)
    line_start(trans_one_all, 2, 0)
    for c in row_reduce:
        c.wait_recv()
    stack_two[q] = reduce_part[r] + reduce_in[0] + (reduce_in[1] + reduce_in[2])
    quad_stack = [over_quad(1, stack_two.at[q], stack_two.at[q], s) for s in range(1, FAN)]
    for c in quad_stack:
        c.start()
    for c in quad_two + row_top:
        c.wait_recv()
    line_wait(couple_two_all, 1, 2)
    line_wait(trans_one_all, 2, 0)
    line_start(trans_one_all, 2, 1)

    couple = split(flat(couple_two_all[...]))
    gain_two = split(dot3(couple, split(flat(trans_two_all[...]))))
    own_two = flat(trans_two_all[q]).T
    for c in quad_stack:
        c.wait_recv()
    solve_two = dot3(couple, split(flat(stack_two[...])))
    top_part[...] = matmul(own_two, solve_two).reshape(FAN, part_rows, part_cols)
    quad_reduce = [
        over_quad(2, top_part.at[(q + s) % FAN], top_in.at[s - 1], s) for s in range(1, FAN)
    ]
    for c in quad_reduce:
        c.start()
    for c in quad_reduce:
        c.wait_recv()
    top_all[sid] = top_part[q] + top_in[0] + (top_in[1] + top_in[2])
    wide_top = [over_wide(top_all.at[sid], top_all.at[sid], s) for s in range(1, wide)]
    for c in wide_top:
        c.start()
    for c in wide_top:
        c.wait_recv()
    total = jnp.zeros((part_rows, part_cols), F32)
    for other in range(groups):
        total = total + matmul(
            flat(top_rows[:, other]), flat(top_all[other * FAN : (other + 1) * FAN])
        )
    block_two[q] = total
    quad_block = [over_quad(3, block_two.at[q], block_two.at[q], s) for s in range(1, FAN)]
    for c in quad_block:
        c.start()
    for c in quad_block:
        c.wait_recv()
    fixed_two_all[r] = solve_two - dot3(gain_two, split(flat(block_two[...])))
    line_start(fixed_two_all, 3, 0)
    line_wait(trans_one_all, 2, 1)
    line_start(trans_one_all, 2, 2)
    line_wait(fixed_two_all, 3, 0)
    line_start(fixed_two_all, 3, 1)
    line_wait(trans_one_all, 2, 2)
    gain_one[...] = matmul(couple_one[...], flat(trans_one_all[...]))
    line_wait(fixed_two_all, 3, 1)
    line_start(fixed_two_all, 3, 2)
    line_wait(fixed_two_all, 3, 2)
    gain = split(gain_one[...])
    for part in range(FAN):
        here = slice(part * part_cols, (part + 1) * part_cols)
        block_out[:, here] = solve_one[:, here] - dot3(gain, split(fixed_two_all[part]))

    for which, buf in enumerate((proj_all, couple_two_all, trans_one_all, fixed_two_all)):
        line_finish(buf, which)
    for c in (
        row_two + tops + quad_two + row_top + row_reduce + quad_stack + quad_reduce
        + wide_top + quad_block
    ):
        c.wait_send()


def last(placed, spread, block, out):
    out[...] = placed[...] - matmul(spread[...], block[...])


def per_device(
    depth,
    groups,
    labels,
    point_order,
    leaf_inverse,
    leaf_basis,
    couple_one,
    transfer_one,
    couple_two,
    transfer_two,
    couple_top,
):
    leaf, cols = labels.shape
    rank = leaf_basis.shape[1]
    part_cols = cols // FAN
    part_rows = rank // FAN
    slice_rows = couple_top.shape[0] // groups
    wide = FAN * groups
    vmem = pl.BlockSpec(memory_space=pltpu.VMEM)
    dma = pltpu.SemaphoreType.DMA
    args = (
        labels, point_order, leaf_inverse, leaf_basis, couple_one, transfer_one,
        couple_two, transfer_two, couple_top,
    )
    placed, spread, block = pl.pallas_call(
        functools.partial(kernel, depth, groups, leaf // 4),
        out_shape=(
            jax.ShapeDtypeStruct((leaf, cols), F32),
            jax.ShapeDtypeStruct((leaf, rank), F32),
            jax.ShapeDtypeStruct((rank, cols), F32),
        ),
        in_specs=[vmem] * len(args),
        out_specs=(vmem, vmem, vmem),
        scratch_shapes=[
            pltpu.VMEM((leaf, cols), BF16),
            pltpu.VMEM((leaf, cols), BF16),
            pltpu.VMEM((2, leaf, cols), BF16),
            pltpu.VMEM((2, leaf, cols), BF16),
            pltpu.VMEM((leaf, 128), jnp.int32),
            pltpu.VMEM((FAN, rank, cols), F32),
            pltpu.VMEM((FAN, *transfer_one.shape), F32),
            pltpu.VMEM((FAN, *couple_two.shape), F32),
            pltpu.VMEM((FAN, rank, part_cols), F32),
            pltpu.VMEM((FAN, rank, part_cols), F32),
            pltpu.VMEM((FAN - 1, rank, part_cols), F32),
            pltpu.VMEM((FAN, rank, part_cols), F32),
            pltpu.VMEM((FAN, FAN, *transfer_two.shape), F32),
            pltpu.VMEM((FAN, part_rows, part_cols), F32),
            pltpu.VMEM((FAN - 1, part_rows, part_cols), F32),
            pltpu.VMEM((wide, part_rows, part_cols), F32),
            pltpu.VMEM((FAN, part_rows, part_cols), F32),
            pltpu.VMEM((FAN, groups, slice_rows, rank), F32),
            pltpu.VMEM((rank, cols), F32),
            pltpu.VMEM((rank, rank), F32),
            dma((4, 2, FAN - 1)),
            dma((4, 2, FAN - 1)),
            dma((3, FAN - 1)),
            dma((3, FAN - 1)),
            dma((4, FAN - 1)),
            dma((4, FAN - 1)),
            dma((wide - 1,)),
            dma((wide - 1,)),
            dma((max(groups - 1, 1),)),
            dma((max(groups - 1, 1),)),
        ],
        compiler_params=pltpu.CompilerParams(
            collective_id=0, has_side_effects=True, vmem_limit_bytes=56 * 1024 * 1024
        ),
    )(*args)
    tile = leaf // 4
    return pl.pallas_call(
        last,
        out_shape=jax.ShapeDtypeStruct((leaf, cols), F32),
        grid=(leaf // tile,),
        in_specs=[
            pl.BlockSpec((tile, cols), lambda i: (i, 0)),
            pl.BlockSpec((tile, rank), lambda i: (i, 0)),
            pl.BlockSpec((rank, cols), lambda i: (0, 0)),
        ],
        out_specs=pl.BlockSpec((tile, cols), lambda i: (i, 0)),
        compiler_params=pltpu.CompilerParams(vmem_limit_bytes=32 * 1024 * 1024),
    )(placed, spread, block)


def solution(mesh):
    depth = mesh.shape["gy"]
    groups = mesh.shape["gx"] * depth // (FAN * FAN)
    spec = P(("gx", "gy"), None)
    return jax.shard_map(
        functools.partial(per_device, depth, groups),
        mesh=mesh,
        in_specs=(spec,) * 9,
        out_specs=spec,
        check_vma=False,
    )
```

```python
import functools

import jax
import jax.numpy as jnp
from jax import lax
from jax.experimental import pallas as pl
from jax.experimental.pallas import tpu as pltpu
from jax.sharding import PartitionSpec as P

F32 = jnp.float32
BF16 = jnp.bfloat16
FAN = 4


def split(x):
    high = x.astype(BF16)
    return high, (x - high.astype(F32)).astype(BF16)


def dot(left, right):
    return jnp.dot(left, right, preferred_element_type=F32)


def dot3(left, right):
    return dot(left[0], right[0]) + (dot(left[0], right[1]) + dot(left[1], right[0]))


def matmul(left, right):
    return dot3(split(left), split(right))


def flat(block):
    return block.reshape(-1, block.shape[-1])


def kernel(
    depth,
    groups,
    tile,
    labels,
    order,
    inverse_hbm,
    basis,
    couple_one,
    transfer_one,
    couple_two,
    transfer_two,
    couple_top,
    placed_hbm,
    spread_hbm,
    block_out,
    placed_out,
    spread_out,
    inverse,
    lab_high,
    lab_low,
    sol_high,
    sol_low,
    column,
    proj_all,
    trans_one_all,
    couple_two_all,
    fixed_two_all,
    reduce_part,
    reduce_in,
    stack_two,
    trans_two_all,
    top_part,
    top_in,
    top_all,
    block_two,
    top_rows,
    solve_one,
    gain_one,
    couple_ward,
    solve_ward,
    gain_ward,
    ward_part,
    pair_send,
    pair_recv,
    local_sem,
    line_send,
    line_recv,
    row_send,
    row_recv,
    quad_send,
    quad_recv,
    wide_send,
    wide_recv,
    tops_send,
    tops_recv,
):
    index = lax.axis_index("gx") * depth + lax.axis_index("gy")
    r = index % FAN
    sid = index // FAN
    q = sid % FAN
    g = sid // FAN
    wide = FAN * groups
    leaf, cols = labels.shape
    rank = basis.shape[1]
    part_cols = cols // FAN
    part_rows = rank // FAN
    slice_rows = couple_top.shape[0] // groups

    mate = r + 1 - 2 * (r % 2)
    inner = jnp.logical_and(r > 0, r < FAN - 1)
    outer = jnp.logical_not(inner)

    def device(sid_of, r_of):
        place = sid_of * FAN + r_of
        return (place // depth, place % depth)

    def copy(source, target, send, recv, where):
        return pltpu.make_async_remote_copy(
            src_ref=source,
            dst_ref=target,
            send_sem=send,
            recv_sem=recv,
            device_id=where,
            device_id_type=pl.DeviceIdType.MESH,
        )

    def line_copy(buf, which, way, step):
        slot = r - step if way == 0 else r + step
        to = r + 1 if way == 0 else r - 1
        slot = jnp.clip(slot, 0, FAN - 1)
        to = jnp.clip(to, 0, FAN - 1)
        return copy(
            buf.at[slot],
            buf.at[slot],
            line_send.at[which, way, step],
            line_recv.at[which, way, step],
            device(sid, to),
        )

    def sends(way, step):
        if way == 0:
            return jnp.logical_and(r >= step, r < FAN - 1)
        return jnp.logical_and(r + step <= FAN - 1, r > 0)

    def receives(way, step):
        if way == 0:
            return r - 1 - step >= 0
        return r + 1 + step <= FAN - 1

    def line_start(buf, which, step):
        for way in range(2):
            @pl.when(sends(way, step))
            def _():
                line_copy(buf, which, way, step).start()

    def line_wait(buf, which, step):
        for way in range(2):
            @pl.when(receives(way, step))
            def _():
                slot = r - 1 - step if way == 0 else r + 1 + step
                slot = jnp.clip(slot, 0, FAN - 1)
                copy(
                    buf.at[slot],
                    buf.at[slot],
                    line_send.at[which, way, step],
                    line_recv.at[which, way, step],
                    device(sid, (r + 1) % FAN),
                ).wait_recv()

    def line_finish(buf, which):
        for step in range(FAN - 1):
            for way in range(2):
                @pl.when(sends(way, step))
                def _():
                    line_copy(buf, which, way, step).wait_send()

    def over_row(which, source, target, step):
        return copy(
            source, target, row_send.at[which, step - 1], row_recv.at[which, step - 1],
            device(sid, (r + step) % FAN),
        )

    def over_quad(which, source, target, step):
        return copy(
            source, target, quad_send.at[which, step - 1], quad_recv.at[which, step - 1],
            device(g * FAN + (q + step) % FAN, r),
        )

    def to_mate(source, target, number):
        return copy(source, target, pair_send.at[number], pair_recv.at[number], device(sid, mate))

    def to_partner(source, target, number):
        return copy(
            source, target, pair_send.at[number], pair_recv.at[number], device(sid, FAN - 1 - r)
        )

    def over_wide(source, target, step):
        return copy(
            source, target, wide_send.at[step - 1], wide_recv.at[step - 1],
            device((sid + step) % wide, r),
        )

    def over_tops(source, target, step):
        return copy(
            source, target, tops_send.at[step - 1], tops_recv.at[step - 1],
            device((g + step) % groups * FAN + q, r),
        )

    barrier = pltpu.get_barrier_semaphore()
    for step in range(1, FAN):
        pl.semaphore_signal(
            barrier, inc=1, device_id=device(sid, (r + step) % FAN),
            device_id_type=pl.DeviceIdType.MESH,
        )
    for step in range(1, wide):
        pl.semaphore_signal(
            barrier, inc=1, device_id=device((sid + step) % wide, r),
            device_id_type=pl.DeviceIdType.MESH,
        )
    pl.semaphore_wait(barrier, FAN - 1 + wide - 1)

    proj_end = to_mate(proj_all.at[r], proj_all.at[r], 0)
    proj_from = to_mate(proj_all.at[mate], proj_all.at[mate], 0)
    couple_end = [
        to_mate(couple_one.at[pl.ds(i * part_rows, part_rows)],
                couple_ward.at[pl.ds(i * part_rows, part_rows)], 1 + i)
        for i in range(FAN)
    ]
    trans_end = to_mate(trans_one_all.at[r], trans_one_all.at[r], 5)
    trans_from = to_mate(trans_one_all.at[mate], trans_one_all.at[mate], 5)
    proj_over = to_partner(proj_all.at[r], proj_all.at[r], 6)
    proj_pass = to_partner(proj_all.at[mate], proj_all.at[mate], 7)
    trans_over = to_partner(trans_one_all.at[r], trans_one_all.at[r], 8)
    trans_pass = to_partner(trans_one_all.at[mate], trans_one_all.at[mate], 9)
    reduce_over = to_partner(
        reduce_part.at[pl.ds((1 - r // 2) * 2, 2)], reduce_in, 10
    )
    reduce_ward = to_mate(ward_part, stack_two.at[q], 11)
    solve_back = to_mate(solve_ward, solve_one, 12)
    gain_back = to_mate(gain_ward, gain_one, 13)

    inverse_load = pltpu.make_async_copy(inverse_hbm, inverse, local_sem.at[0])
    inverse_load.start()
    width = couple_two.shape[1]
    couple_two_all[r, :, :width] = couple_two[...]
    couple_two_all[r, :, width:] = transfer_two[...]
    trans_one_all[r] = transfer_one[...]
    top_rows[r, g] = couple_top[pl.ds(pl.multiple_of(g * slice_rows, slice_rows), slice_rows), :]
    line_start(couple_two_all, 0, 0)

    @pl.when(outer)
    def _():
        couple_end[0].start()

    tops = []
    for s in range(1, groups):
        other = (g + s) % groups
        tops.append(
            over_tops(
                couple_top.at[pl.ds(pl.multiple_of(other * slice_rows, slice_rows), slice_rows)],
                top_rows.at[r, g],
                s,
            )
        )
        tops[-1].start()

    lab_high[...], lab_low[...] = split(labels[...])
    position = jnp.broadcast_to(order[...].astype(F32), (128, leaf)).T
    column[...] = position.astype(jnp.int32)
    rhs_high, rhs_low = placed_high, placed_low = sol_high.at[0], sol_low.at[0]
    sol_h, sol_l = sol_high.at[1], sol_low.at[1]
    tiles = leaf // tile

    def rows_of(step):
        return pl.ds(pl.multiple_of(step * tile, tile), tile)

    @pl.loop(0, tiles)
    def _(step):
        rows = rows_of(step)
        hot = column[rows, 0:1] == lax.broadcasted_iota(jnp.int32, (tile, leaf), 1)
        hot = hot.astype(F32).astype(BF16)
        rhs_high[rows, :] = dot(hot, lab_high[...]).astype(BF16)
        rhs_low[rows, :] = dot(hot, lab_low[...]).astype(BF16)

    inverse_load.wait()

    @pl.loop(0, tiles)
    def _(step):
        rows = rows_of(step)
        value = dot3(split(inverse[rows, :]), (rhs_high[...], rhs_low[...]))
        sol_h[rows, :], sol_l[rows, :] = split(value)

    proj_all[r] = dot3(split(basis[...].T), (sol_h[...], sol_l[...]))

    @pl.when(outer)
    def _():
        proj_end.start()

    @pl.when(inner)
    def _():
        proj_over.start()

    basis_parts = split(basis[...])
    lab_high[:, :rank], lab_low[:, :rank] = basis_parts

    @pl.loop(0, tiles)
    def _(step):
        rows = rows_of(step)
        value = dot3(split(inverse[rows, :]), (lab_high[:, :rank], lab_low[:, :rank]))
        rhs_high[rows, :rank], rhs_low[rows, :rank] = split(value)


    @pl.loop(0, tiles)
    def _(step):
        rows = rows_of(step)
        hot = (lax.broadcasted_iota(jnp.int32, (tile, leaf), 0) + step * tile) == order[...]
        hot = hot.astype(F32).astype(BF16)
        placed_out[rows, :] = dot(hot, sol_h[...]) + dot(hot, sol_l[...])
        spread_out[rows, :] = dot(hot, rhs_high[:, :rank]) + dot(hot, rhs_low[:, :rank])

    placed_store = pltpu.make_async_copy(placed_out, placed_hbm, local_sem.at[1])
    spread_store = pltpu.make_async_copy(spread_out, spread_hbm, local_sem.at[2])
    placed_store.start()
    spread_store.start()

    for c in tops:
        c.wait_recv()
    row_top = [over_row(0, top_rows.at[r], top_rows.at[r], s) for s in range(1, FAN)]

    @pl.when(outer)
    def _():
        proj_end.wait_send()
        for c in couple_end[1:]:
            c.start()
        trans_end.start()

    @pl.when(inner)
    def _():
        proj_from.wait_recv()
        proj_pass.start()
        proj_over.wait_recv()
        proj_pass.wait_recv()

    line_wait(couple_two_all, 0, 0)
    line_start(couple_two_all, 0, 1)
    for c in row_top:
        c.start()

    @pl.when(inner)
    def _():
        stack_one = split(flat(proj_all[...]))
        solve_one[...] = dot3(split(couple_one[...]), stack_one)
        for c in couple_end:
            c.wait_recv()
        solve_ward[...] = dot3(split(couple_ward[...]), stack_one)
        trans_from.wait_recv()
        reduced = matmul(transfer_one[...].T, solve_one[...]) + matmul(
            trans_one_all[mate].T, solve_ward[...]
        )
        for part in range(FAN):
            reduce_part[part] = reduced[:, part * part_cols : (part + 1) * part_cols]
        reduce_over.start()
        reduce_over.wait_recv()
        ward_part[...] = reduce_part[mate] + reduce_in[mate % 2]
        reduce_ward.start()
        stack_two[q] = reduce_part[r] + reduce_in[r % 2]

    @pl.when(outer)
    def _():
        reduce_ward.wait_recv()

    quad_stack = [over_quad(1, stack_two.at[q], stack_two.at[q], s) for s in range(1, FAN)]
    for c in quad_stack:
        c.start()

    line_wait(couple_two_all, 0, 1)
    line_start(couple_two_all, 0, 2)

    @pl.when(inner)
    def _():
        solve_back.start()
        trans_over.start()
        trans_pass.start()

    line_wait(couple_two_all, 0, 2)
    trans_two_all[q] = couple_two_all[:, :, width:]
    quad_two = [
        over_quad(0, trans_two_all.at[q], trans_two_all.at[q], s) for s in range(1, FAN)
    ]
    for c in quad_two:
        c.start()
    for c in row_top:
        c.wait_recv()

    couple = split(flat(couple_two_all[:, :, :width]))
    own_two = flat(trans_two_all[q]).T
    for c in quad_stack:
        c.wait_recv()
    solve_two = dot3(couple, split(flat(stack_two[...])))
    top_part[...] = matmul(own_two, solve_two).reshape(FAN, part_rows, part_cols)
    quad_reduce = [
        over_quad(2, top_part.at[(q + s) % FAN], top_in.at[s - 1], s) for s in range(1, FAN)
    ]
    for c in quad_reduce:
        c.start()
    for c in quad_two:
        c.wait_recv()
    gain_two = split(dot3(couple, split(flat(trans_two_all[...]))))
    for c in quad_reduce:
        c.wait_recv()
    top_all[sid] = top_part[q] + top_in[0] + (top_in[1] + top_in[2])
    wide_top = [over_wide(top_all.at[sid], top_all.at[sid], s) for s in range(1, wide)]
    for c in wide_top:
        c.start()
    for c in wide_top:
        c.wait_recv()
    total = jnp.zeros((part_rows, part_cols), F32)
    for other in range(groups):
        total = total + matmul(
            flat(top_rows[:, other]), flat(top_all[other * FAN : (other + 1) * FAN])
        )
    block_two[q] = total
    quad_block = [over_quad(3, block_two.at[q], block_two.at[q], s) for s in range(1, FAN)]
    for c in quad_block:
        c.start()
    for c in quad_block:
        c.wait_recv()
    fixed_two_all[r] = solve_two - dot3(gain_two, split(flat(block_two[...])))
    line_start(fixed_two_all, 1, 0)

    @pl.when(inner)
    def _():
        trans_over.wait_recv()
        trans_pass.wait_recv()
        trans_full = split(flat(trans_one_all[...]))
        gain_ward[...] = dot3(split(couple_ward[...]), trans_full)
        gain_back.start()
        gain_one[...] = dot3(split(couple_one[...]), trans_full)

    line_wait(fixed_two_all, 1, 0)
    line_start(fixed_two_all, 1, 1)
    line_wait(fixed_two_all, 1, 1)
    line_start(fixed_two_all, 1, 2)
    line_wait(fixed_two_all, 1, 2)

    @pl.when(outer)
    def _():
        solve_back.wait_recv()
        gain_back.wait_recv()

    gain = split(gain_one[...])
    for part in range(FAN):
        here = slice(part * part_cols, (part + 1) * part_cols)
        block_out[:, here] = solve_one[:, here] - dot3(gain, split(fixed_two_all[part]))

    for which, buf in enumerate((couple_two_all, fixed_two_all)):
        line_finish(buf, which)

    @pl.when(outer)
    def _():
        for c in couple_end:
            c.wait_send()
        trans_end.wait_send()

    @pl.when(inner)
    def _():
        for c in (
            proj_over, proj_pass, trans_over, trans_pass, reduce_over, reduce_ward,
            solve_back, gain_back,
        ):
            c.wait_send()

    for c in tops + row_top + quad_two + quad_stack + quad_reduce + wide_top + quad_block:
        c.wait_send()
    placed_store.wait()
    spread_store.wait()


def last(placed, spread, block, out):
    out[...] = placed[...] - matmul(spread[...], block[...])


def per_device(
    depth,
    groups,
    labels,
    point_order,
    leaf_inverse,
    leaf_basis,
    couple_one,
    transfer_one,
    couple_two,
    transfer_two,
    couple_top,
):
    leaf, cols = labels.shape
    rank = leaf_basis.shape[1]
    part_cols = cols // FAN
    part_rows = rank // FAN
    slice_rows = couple_top.shape[0] // groups
    wide = FAN * groups
    vmem = pl.BlockSpec(memory_space=pltpu.VMEM)
    far = pl.BlockSpec(memory_space=pl.ANY)
    dma = pltpu.SemaphoreType.DMA
    args = (
        labels, point_order, leaf_inverse, leaf_basis, couple_one, transfer_one,
        couple_two, transfer_two, couple_top,
    )
    placed, spread, block = pl.pallas_call(
        functools.partial(kernel, depth, groups, leaf // 4),
        out_shape=(
            jax.ShapeDtypeStruct((leaf, cols), F32),
            jax.ShapeDtypeStruct((leaf, rank), F32),
            jax.ShapeDtypeStruct((rank, cols), F32),
        ),
        in_specs=[vmem, vmem, far] + [vmem] * (len(args) - 3),
        out_specs=(far, far, vmem),
        scratch_shapes=[
            pltpu.VMEM((leaf, cols), F32),
            pltpu.VMEM((leaf, rank), F32),
            pltpu.VMEM((leaf, leaf), F32),
            pltpu.VMEM((leaf, cols), BF16),
            pltpu.VMEM((leaf, cols), BF16),
            pltpu.VMEM((2, leaf, cols), BF16),
            pltpu.VMEM((2, leaf, cols), BF16),
            pltpu.VMEM((leaf, 128), jnp.int32),
            pltpu.VMEM((FAN, rank, cols), F32),
            pltpu.VMEM((FAN, *transfer_one.shape), F32),
            pltpu.VMEM((FAN, couple_two.shape[0], couple_two.shape[1] + rank), F32),
            pltpu.VMEM((FAN, rank, part_cols), F32),
            pltpu.VMEM((FAN, rank, part_cols), F32),
            pltpu.VMEM((2, rank, part_cols), F32),
            pltpu.VMEM((FAN, rank, part_cols), F32),
            pltpu.VMEM((FAN, FAN, *transfer_two.shape), F32),
            pltpu.VMEM((FAN, part_rows, part_cols), F32),
            pltpu.VMEM((FAN - 1, part_rows, part_cols), F32),
            pltpu.VMEM((wide, part_rows, part_cols), F32),
            pltpu.VMEM((FAN, part_rows, part_cols), F32),
            pltpu.VMEM((FAN, groups, slice_rows, rank), F32),
            pltpu.VMEM((rank, cols), F32),
            pltpu.VMEM((rank, rank), F32),
            pltpu.VMEM(couple_one.shape, F32),
            pltpu.VMEM((rank, cols), F32),
            pltpu.VMEM((rank, rank), F32),
            pltpu.VMEM((rank, part_cols), F32),
            dma((14,)),
            dma((14,)),
            dma((3,)),
            dma((2, 2, FAN - 1)),
            dma((2, 2, FAN - 1)),
            dma((1, FAN - 1)),
            dma((1, FAN - 1)),
            dma((4, FAN - 1)),
            dma((4, FAN - 1)),
            dma((wide - 1,)),
            dma((wide - 1,)),
            dma((max(groups - 1, 1),)),
            dma((max(groups - 1, 1),)),
        ],
        compiler_params=pltpu.CompilerParams(
            collective_id=0, has_side_effects=True, vmem_limit_bytes=56 * 1024 * 1024
        ),
    )(*args)
    tile = leaf // 4
    return pl.pallas_call(
        last,
        out_shape=jax.ShapeDtypeStruct((leaf, cols), F32),
        grid=(leaf // tile,),
        in_specs=[
            pl.BlockSpec((tile, cols), lambda i: (i, 0)),
            pl.BlockSpec((tile, rank), lambda i: (i, 0)),
            pl.BlockSpec((rank, cols), lambda i: (0, 0)),
        ],
        out_specs=pl.BlockSpec((tile, cols), lambda i: (i, 0)),
        compiler_params=pltpu.CompilerParams(vmem_limit_bytes=60 * 1024 * 1024),
    )(placed, spread, block)


def solution(mesh):
    depth = mesh.shape["gy"]
    groups = mesh.shape["gx"] * depth // (FAN * FAN)
    spec = P(("gx", "gy"), None)
    return jax.shard_map(
        functools.partial(per_device, depth, groups),
        mesh=mesh,
        in_specs=(spec,) * 9,
        out_specs=spec,
        check_vma=False,
    )
```

```python
import functools

import jax
import jax.numpy as jnp
from jax import lax
from jax.experimental import pallas as pl
from jax.experimental.pallas import tpu as pltpu
from jax.sharding import PartitionSpec as P

F32 = jnp.float32
BF16 = jnp.bfloat16
FAN = 4
TILES = 1


def split(x):
    high = x.astype(BF16)
    return high, (x - high.astype(F32)).astype(BF16)


def dot(left, right):
    return jnp.dot(left, right, preferred_element_type=F32)


def dot3(left, right):
    return dot(left[0], right[0]) + (dot(left[0], right[1]) + dot(left[1], right[0]))


def matmul(left, right):
    return dot3(split(left), split(right))


def flat(block):
    return block.reshape(-1, block.shape[-1])


def kernel(
    depth,
    groups,
    tile,
    labels,
    order,
    inverse_hbm,
    basis,
    couple_one,
    transfer_one,
    couple_two,
    transfer_two,
    couple_top,
    placed_hbm,
    spread_hbm,
    block_out,
    placed_out,
    spread_out,
    inverse,
    lab_high,
    lab_low,
    sol_high,
    sol_low,
    column,
    proj_all,
    trans_one_all,
    couple_two_all,
    fixed_two_all,
    reduce_part,
    reduce_in,
    stack_two,
    trans_two_all,
    top_part,
    top_in,
    top_all,
    block_two,
    top_rows,
    solve_one,
    gain_one,
    couple_ward,
    solve_ward,
    gain_ward,
    ward_part,
    pair_send,
    pair_recv,
    local_sem,
    line_send,
    line_recv,
    row_send,
    row_recv,
    quad_send,
    quad_recv,
    wide_send,
    wide_recv,
    tops_send,
    tops_recv,
):
    index = lax.axis_index("gx") * depth + lax.axis_index("gy")
    r = index % FAN
    sid = index // FAN
    q = sid % FAN
    g = sid // FAN
    wide = FAN * groups
    leaf, cols = labels.shape
    rank = basis.shape[1]
    part_cols = cols // FAN
    part_rows = rank // FAN
    slice_rows = couple_top.shape[0] // groups

    mate = r + 1 - 2 * (r % 2)
    inner = jnp.logical_and(r > 0, r < FAN - 1)
    outer = jnp.logical_not(inner)

    def device(sid_of, r_of):
        place = sid_of * FAN + r_of
        return (place // depth, place % depth)

    def copy(source, target, send, recv, where):
        return pltpu.make_async_remote_copy(
            src_ref=source,
            dst_ref=target,
            send_sem=send,
            recv_sem=recv,
            device_id=where,
            device_id_type=pl.DeviceIdType.MESH,
        )

    def line_copy(buf, which, way, step):
        slot = r - step if way == 0 else r + step
        to = r + 1 if way == 0 else r - 1
        slot = jnp.clip(slot, 0, FAN - 1)
        to = jnp.clip(to, 0, FAN - 1)
        return copy(
            buf.at[slot],
            buf.at[slot],
            line_send.at[which, way, step],
            line_recv.at[which, way, step],
            device(sid, to),
        )

    def sends(way, step):
        if way == 0:
            return jnp.logical_and(r >= step, r < FAN - 1)
        return jnp.logical_and(r + step <= FAN - 1, r > 0)

    def receives(way, step):
        if way == 0:
            return r - 1 - step >= 0
        return r + 1 + step <= FAN - 1

    def line_start(buf, which, step):
        for way in range(2):
            @pl.when(sends(way, step))
            def _():
                line_copy(buf, which, way, step).start()

    def line_wait(buf, which, step):
        for way in range(2):
            @pl.when(receives(way, step))
            def _():
                slot = r - 1 - step if way == 0 else r + 1 + step
                slot = jnp.clip(slot, 0, FAN - 1)
                copy(
                    buf.at[slot],
                    buf.at[slot],
                    line_send.at[which, way, step],
                    line_recv.at[which, way, step],
                    device(sid, (r + 1) % FAN),
                ).wait_recv()

    def line_finish(buf, which):
        for step in range(FAN - 1):
            for way in range(2):
                @pl.when(sends(way, step))
                def _():
                    line_copy(buf, which, way, step).wait_send()

    def over_row(which, source, target, step):
        return copy(
            source, target, row_send.at[which, step - 1], row_recv.at[which, step - 1],
            device(sid, (r + step) % FAN),
        )

    def over_quad(which, source, target, step):
        return copy(
            source, target, quad_send.at[which, step - 1], quad_recv.at[which, step - 1],
            device(g * FAN + (q + step) % FAN, r),
        )

    def to_mate(source, target, number):
        return copy(source, target, pair_send.at[number], pair_recv.at[number], device(sid, mate))

    def to_partner(source, target, number):
        return copy(
            source, target, pair_send.at[number], pair_recv.at[number], device(sid, FAN - 1 - r)
        )

    def over_wide(source, target, step):
        return copy(
            source, target, wide_send.at[step - 1], wide_recv.at[step - 1],
            device((sid + step) % wide, r),
        )

    def over_tops(source, target, step):
        return copy(
            source, target, tops_send.at[step - 1], tops_recv.at[step - 1],
            device((g + step) % groups * FAN + q, r),
        )

    barrier = pltpu.get_barrier_semaphore()
    for step in range(1, FAN):
        pl.semaphore_signal(
            barrier, inc=1, device_id=device(sid, (r + step) % FAN),
            device_id_type=pl.DeviceIdType.MESH,
        )
    for step in range(1, wide):
        pl.semaphore_signal(
            barrier, inc=1, device_id=device((sid + step) % wide, r),
            device_id_type=pl.DeviceIdType.MESH,
        )
    pl.semaphore_wait(barrier, FAN - 1 + wide - 1)

    proj_end = to_mate(proj_all.at[r], proj_all.at[r], 0)
    proj_from = to_mate(proj_all.at[mate], proj_all.at[mate], 0)
    couple_end = [
        to_mate(couple_one.at[pl.ds(i * part_rows, part_rows)],
                couple_ward.at[pl.ds(i * part_rows, part_rows)], 1 + i)
        for i in range(FAN)
    ]
    trans_end = to_mate(trans_one_all.at[r], trans_one_all.at[r], 5)
    trans_from = to_mate(trans_one_all.at[mate], trans_one_all.at[mate], 5)
    proj_over = to_partner(proj_all.at[r], proj_all.at[r], 6)
    proj_pass = to_partner(proj_all.at[mate], proj_all.at[mate], 7)
    trans_over = to_partner(trans_one_all.at[r], trans_one_all.at[r], 8)
    trans_pass = to_partner(trans_one_all.at[mate], trans_one_all.at[mate], 9)
    reduce_over = to_partner(
        reduce_part.at[pl.ds((1 - r // 2) * 2, 2)], reduce_in, 10
    )
    reduce_ward = to_mate(ward_part, stack_two.at[q], 11)
    solve_back = to_mate(solve_ward, solve_one, 12)
    gain_back = to_mate(gain_ward, gain_one, 13)

    two_end = to_mate(couple_two_all.at[r], couple_two_all.at[r], 14)
    two_from = to_mate(couple_two_all.at[mate], couple_two_all.at[mate], 14)
    two_over = to_partner(couple_two_all.at[r], couple_two_all.at[r], 15)
    two_pass = to_partner(couple_two_all.at[mate], couple_two_all.at[mate], 16)
    across, beyond = FAN - 1 - r, FAN - 1 - mate
    two_own = to_mate(couple_two_all.at[r], couple_two_all.at[r], 17)
    two_across = to_mate(couple_two_all.at[across], couple_two_all.at[across], 18)
    two_beyond = to_mate(couple_two_all.at[beyond], couple_two_all.at[beyond], 19)

    inverse_load = pltpu.make_async_copy(inverse_hbm, inverse, local_sem.at[0])
    inverse_load.start()
    width = couple_two.shape[1]
    couple_two_all[r, :, :width] = couple_two[...]
    couple_two_all[r, :, width:] = transfer_two[...]
    trans_one_all[r] = transfer_one[...]
    top_rows[r, g] = couple_top[pl.ds(pl.multiple_of(g * slice_rows, slice_rows), slice_rows), :]

    @pl.when(outer)
    def _():
        trans_end.start()
        for c in couple_end[:2]:
            c.start()

    @pl.when(inner)
    def _():
        two_over.start()
        two_own.start()

    tops = []
    for s in range(1, groups):
        other = (g + s) % groups
        tops.append(
            over_tops(
                couple_top.at[pl.ds(pl.multiple_of(other * slice_rows, slice_rows), slice_rows)],
                top_rows.at[r, g],
                s,
            )
        )
        tops[-1].start()

    lab_high[...], lab_low[...] = split(labels[...])
    position = jnp.broadcast_to(order[...].astype(F32), (128, leaf)).T
    column[...] = position.astype(jnp.int32)
    rhs_high, rhs_low = placed_high, placed_low = sol_high.at[0], sol_low.at[0]
    sol_h, sol_l = sol_high.at[1], sol_low.at[1]
    tiles = leaf // tile

    def rows_of(step):
        return pl.ds(pl.multiple_of(step * tile, tile), tile)

    @pl.loop(0, tiles)
    def _(step):
        rows = rows_of(step)
        hot = column[rows, 0:1] == lax.broadcasted_iota(jnp.int32, (tile, leaf), 1)
        hot = hot.astype(F32).astype(BF16)
        rhs_high[rows, :] = dot(hot, lab_high[...]).astype(BF16)
        rhs_low[rows, :] = dot(hot, lab_low[...]).astype(BF16)

    inverse_load.wait()

    @pl.loop(0, tiles)
    def _(step):
        rows = rows_of(step)
        value = dot3(split(inverse[rows, :]), (rhs_high[...], rhs_low[...]))
        sol_h[rows, :], sol_l[rows, :] = split(value)

    proj_all[r] = dot3(split(basis[...].T), (sol_h[...], sol_l[...]))

    @pl.when(outer)
    def _():
        proj_end.start()

    @pl.when(inner)
    def _():
        proj_over.start()

    basis_parts = split(basis[...])
    lab_high[:, :rank], lab_low[:, :rank] = basis_parts

    @pl.loop(0, tiles)
    def _(step):
        rows = rows_of(step)
        value = dot3(split(inverse[rows, :]), (lab_high[:, :rank], lab_low[:, :rank]))
        rhs_high[rows, :rank], rhs_low[rows, :rank] = split(value)


    @pl.loop(0, tiles)
    def _(step):
        rows = rows_of(step)
        hot = (lax.broadcasted_iota(jnp.int32, (tile, leaf), 0) + step * tile) == order[...]
        hot = hot.astype(F32).astype(BF16)
        placed_out[rows, :] = dot(hot, sol_h[...]) + dot(hot, sol_l[...])
        spread_out[rows, :] = dot(hot, rhs_high[:, :rank]) + dot(hot, rhs_low[:, :rank])

    placed_store = pltpu.make_async_copy(placed_out, placed_hbm, local_sem.at[1])
    spread_store = pltpu.make_async_copy(spread_out, spread_hbm, local_sem.at[2])
    placed_store.start()
    spread_store.start()

    for c in tops:
        c.wait_recv()
    row_top = [over_row(0, top_rows.at[r], top_rows.at[r], s) for s in range(1, FAN)]

    @pl.when(outer)
    def _():
        proj_end.wait_send()
        for c in couple_end[2:]:
            c.start()
        two_end.start()

    @pl.when(inner)
    def _():
        two_over.wait_recv()
        two_across.start()
        proj_from.wait_recv()
        proj_pass.start()
        proj_over.wait_recv()
        proj_pass.wait_recv()

    for c in row_top:
        c.start()

    @pl.when(inner)
    def _():
        stack_one = split(flat(proj_all[...]))
        solve_one[...] = dot3(split(couple_one[...]), stack_one)
        reduced = matmul(transfer_one[...].T, solve_one[...])
        for c in couple_end:
            c.wait_recv()
        trans_from.wait_recv()
        solve_ward[...] = dot3(split(couple_ward[...]), stack_one)
        reduced = reduced + matmul(trans_one_all[mate].T, solve_ward[...])
        for part in range(FAN):
            reduce_part[part] = reduced[:, part * part_cols : (part + 1) * part_cols]
        reduce_over.start()
        reduce_over.wait_recv()
        ward_part[...] = reduce_part[mate] + reduce_in[mate % 2]
        reduce_ward.start()
        stack_two[q] = reduce_part[r] + reduce_in[r % 2]

    @pl.when(outer)
    def _():
        reduce_ward.wait_recv()

    quad_stack = [over_quad(1, stack_two.at[q], stack_two.at[q], s) for s in range(1, FAN)]
    for c in quad_stack:
        c.start()

    @pl.when(inner)
    def _():
        two_from.wait_recv()
        two_pass.start()
        trans_over.start()
        trans_pass.start()
        two_pass.wait_recv()
        two_beyond.start()
        solve_back.start()

    @pl.when(outer)
    def _():
        two_own.wait_recv()
        two_across.wait_recv()
        two_beyond.wait_recv()

    trans_two_all[q] = couple_two_all[:, :, width:]
    quad_two = [
        over_quad(0, trans_two_all.at[q], trans_two_all.at[q], s) for s in range(1, FAN)
    ]
    for c in quad_two:
        c.start()
    for c in row_top:
        c.wait_recv()

    couple = split(flat(couple_two_all[:, :, :width]))
    own_two = flat(trans_two_all[q]).T
    for c in quad_stack:
        c.wait_recv()
    solve_two = dot3(couple, split(flat(stack_two[...])))
    top_part[...] = matmul(own_two, solve_two).reshape(FAN, part_rows, part_cols)
    quad_reduce = [
        over_quad(2, top_part.at[(q + s) % FAN], top_in.at[s - 1], s) for s in range(1, FAN)
    ]
    for c in quad_reduce:
        c.start()
    for c in quad_two:
        c.wait_recv()
    gain_two = split(dot3(couple, split(flat(trans_two_all[...]))))
    for c in quad_reduce:
        c.wait_recv()
    top_all[sid] = top_part[q] + top_in[0] + (top_in[1] + top_in[2])
    wide_top = [over_wide(top_all.at[sid], top_all.at[sid], s) for s in range(1, wide)]
    for c in wide_top:
        c.start()
    for c in wide_top:
        c.wait_recv()
    total = jnp.zeros((part_rows, part_cols), F32)
    for other in range(groups):
        total = total + matmul(
            flat(top_rows[:, other]), flat(top_all[other * FAN : (other + 1) * FAN])
        )
    block_two[q] = total
    quad_block = [over_quad(3, block_two.at[q], block_two.at[q], s) for s in range(1, FAN)]
    for c in quad_block:
        c.start()
    for c in quad_block:
        c.wait_recv()
    fixed_two_all[r] = solve_two - dot3(gain_two, split(flat(block_two[...])))
    line_start(fixed_two_all, 0, 0)

    @pl.when(inner)
    def _():
        trans_over.wait_recv()
        trans_pass.wait_recv()
        trans_full = split(flat(trans_one_all[...]))
        gain_ward[...] = dot3(split(couple_ward[...]), trans_full)
        gain_back.start()
        gain_one[...] = dot3(split(couple_one[...]), trans_full)

    line_wait(fixed_two_all, 0, 0)
    line_start(fixed_two_all, 0, 1)
    line_wait(fixed_two_all, 0, 1)
    line_start(fixed_two_all, 0, 2)
    line_wait(fixed_two_all, 0, 2)

    @pl.when(outer)
    def _():
        solve_back.wait_recv()
        gain_back.wait_recv()

    gain = split(gain_one[...])
    for part in range(FAN):
        here = slice(part * part_cols, (part + 1) * part_cols)
        block_out[:, here] = solve_one[:, here] - dot3(gain, split(fixed_two_all[part]))

    for which, buf in enumerate((fixed_two_all,)):
        line_finish(buf, which)

    @pl.when(outer)
    def _():
        for c in couple_end:
            c.wait_send()
        trans_end.wait_send()
        two_end.wait_send()

    @pl.when(inner)
    def _():
        for c in (
            proj_over, proj_pass, trans_over, trans_pass, reduce_over, reduce_ward,
            solve_back, gain_back, two_over, two_pass, two_own, two_across, two_beyond,
        ):
            c.wait_send()

    for c in tops + row_top + quad_two + quad_stack + quad_reduce + wide_top + quad_block:
        c.wait_send()
    placed_store.wait()
    spread_store.wait()


def per_device(
    depth,
    groups,
    labels,
    point_order,
    leaf_inverse,
    leaf_basis,
    couple_one,
    transfer_one,
    couple_two,
    transfer_two,
    couple_top,
):
    leaf, cols = labels.shape
    rank = leaf_basis.shape[1]
    part_cols = cols // FAN
    part_rows = rank // FAN
    slice_rows = couple_top.shape[0] // groups
    wide = FAN * groups
    vmem = pl.BlockSpec(memory_space=pltpu.VMEM)
    far = pl.BlockSpec(memory_space=pl.ANY)
    dma = pltpu.SemaphoreType.DMA
    args = (
        labels, point_order, leaf_inverse, leaf_basis, couple_one, transfer_one,
        couple_two, transfer_two, couple_top,
    )
    placed, spread, block = pl.pallas_call(
        functools.partial(kernel, depth, groups, leaf // TILES),
        out_shape=(
            jax.ShapeDtypeStruct((leaf, cols), F32),
            jax.ShapeDtypeStruct((leaf, rank), F32),
            jax.ShapeDtypeStruct((rank, cols), F32),
        ),
        in_specs=[vmem, vmem, far] + [vmem] * (len(args) - 3),
        out_specs=(far, far, vmem),
        scratch_shapes=[
            pltpu.VMEM((leaf, cols), F32),
            pltpu.VMEM((leaf, rank), F32),
            pltpu.VMEM((leaf, leaf), F32),
            pltpu.VMEM((leaf, cols), BF16),
            pltpu.VMEM((leaf, cols), BF16),
            pltpu.VMEM((2, leaf, cols), BF16),
            pltpu.VMEM((2, leaf, cols), BF16),
            pltpu.VMEM((leaf, 128), jnp.int32),
            pltpu.VMEM((FAN, rank, cols), F32),
            pltpu.VMEM((FAN, *transfer_one.shape), F32),
            pltpu.VMEM((FAN, couple_two.shape[0], couple_two.shape[1] + rank), F32),
            pltpu.VMEM((FAN, rank, part_cols), F32),
            pltpu.VMEM((FAN, rank, part_cols), F32),
            pltpu.VMEM((2, rank, part_cols), F32),
            pltpu.VMEM((FAN, rank, part_cols), F32),
            pltpu.VMEM((FAN, FAN, *transfer_two.shape), F32),
            pltpu.VMEM((FAN, part_rows, part_cols), F32),
            pltpu.VMEM((FAN - 1, part_rows, part_cols), F32),
            pltpu.VMEM((wide, part_rows, part_cols), F32),
            pltpu.VMEM((FAN, part_rows, part_cols), F32),
            pltpu.VMEM((FAN, groups, slice_rows, rank), F32),
            pltpu.VMEM((rank, cols), F32),
            pltpu.VMEM((rank, rank), F32),
            pltpu.VMEM(couple_one.shape, F32),
            pltpu.VMEM((rank, cols), F32),
            pltpu.VMEM((rank, rank), F32),
            pltpu.VMEM((rank, part_cols), F32),
            dma((20,)),
            dma((20,)),
            dma((3,)),
            dma((1, 2, FAN - 1)),
            dma((1, 2, FAN - 1)),
            dma((1, FAN - 1)),
            dma((1, FAN - 1)),
            dma((4, FAN - 1)),
            dma((4, FAN - 1)),
            dma((wide - 1,)),
            dma((wide - 1,)),
            dma((max(groups - 1, 1),)),
            dma((max(groups - 1, 1),)),
        ],
        compiler_params=pltpu.CompilerParams(
            collective_id=0, has_side_effects=True, vmem_limit_bytes=56 * 1024 * 1024
        ),
    )(*args)
    return placed - jnp.dot(spread, block, precision=lax.Precision.HIGH)


def solution(mesh):
    depth = mesh.shape["gy"]
    groups = mesh.shape["gx"] * depth // (FAN * FAN)
    spec = P(("gx", "gy"), None)
    return jax.shard_map(
        functools.partial(per_device, depth, groups),
        mesh=mesh,
        in_specs=(spec,) * 9,
        out_specs=spec,
        check_vma=False,
    )
```

```python
import functools

import jax
import jax.numpy as jnp
from jax import lax
from jax.experimental import pallas as pl
from jax.experimental.pallas import tpu as pltpu
from jax.sharding import PartitionSpec as P

F32 = jnp.float32
BF16 = jnp.bfloat16
FAN = 4
TILES = 2


def split(x):
    high = x.astype(BF16)
    return high, (x - high.astype(F32)).astype(BF16)


def dot(left, right):
    return jnp.dot(left, right, preferred_element_type=F32)


def dot3(left, right):
    return dot(left[0], right[0]) + (dot(left[0], right[1]) + dot(left[1], right[0]))


def matmul(left, right):
    return dot3(split(left), split(right))


def flat(block):
    return block.reshape(-1, block.shape[-1])


def kernel(
    depth,
    groups,
    tile,
    labels,
    order,
    inverse_hbm,
    basis,
    couple_one,
    transfer_one,
    couple_two,
    transfer_two,
    couple_top,
    placed_hbm,
    spread_hbm,
    block_out,
    placed_out,
    spread_out,
    inverse,
    lab_high,
    lab_low,
    sol_high,
    sol_low,
    column,
    proj_all,
    trans_one_all,
    couple_two_all,
    fixed_two_all,
    reduce_part,
    reduce_in,
    stack_two,
    trans_two_all,
    top_part,
    top_in,
    top_all,
    block_two,
    top_rows,
    solve_one,
    gain_one,
    couple_ward,
    solve_ward,
    gain_ward,
    ward_part,
    pair_send,
    pair_recv,
    local_sem,
    line_send,
    line_recv,
    row_send,
    row_recv,
    quad_send,
    quad_recv,
    wide_send,
    wide_recv,
    tops_send,
    tops_recv,
):
    index = lax.axis_index("gx") * depth + lax.axis_index("gy")
    r = index % FAN
    sid = index // FAN
    q = sid % FAN
    g = sid // FAN
    wide = FAN * groups
    leaf, cols = labels.shape
    rank = basis.shape[1]
    part_cols = cols // FAN
    part_rows = rank // FAN
    slice_rows = couple_top.shape[0] // groups

    mate = r + 1 - 2 * (r % 2)
    inner = jnp.logical_and(r > 0, r < FAN - 1)
    outer = jnp.logical_not(inner)

    def device(sid_of, r_of):
        place = sid_of * FAN + r_of
        return (place // depth, place % depth)

    def copy(source, target, send, recv, where):
        return pltpu.make_async_remote_copy(
            src_ref=source,
            dst_ref=target,
            send_sem=send,
            recv_sem=recv,
            device_id=where,
            device_id_type=pl.DeviceIdType.MESH,
        )

    def line_copy(buf, which, way, step):
        slot = r - step if way == 0 else r + step
        to = r + 1 if way == 0 else r - 1
        slot = jnp.clip(slot, 0, FAN - 1)
        to = jnp.clip(to, 0, FAN - 1)
        return copy(
            buf.at[slot],
            buf.at[slot],
            line_send.at[which, way, step],
            line_recv.at[which, way, step],
            device(sid, to),
        )

    def sends(way, step):
        if way == 0:
            return jnp.logical_and(r >= step, r < FAN - 1)
        return jnp.logical_and(r + step <= FAN - 1, r > 0)

    def receives(way, step):
        if way == 0:
            return r - 1 - step >= 0
        return r + 1 + step <= FAN - 1

    def line_start(buf, which, step):
        for way in range(2):
            @pl.when(sends(way, step))
            def _():
                line_copy(buf, which, way, step).start()

    def line_wait(buf, which, step):
        for way in range(2):
            @pl.when(receives(way, step))
            def _():
                slot = r - 1 - step if way == 0 else r + 1 + step
                slot = jnp.clip(slot, 0, FAN - 1)
                copy(
                    buf.at[slot],
                    buf.at[slot],
                    line_send.at[which, way, step],
                    line_recv.at[which, way, step],
                    device(sid, (r + 1) % FAN),
                ).wait_recv()

    def line_finish(buf, which):
        for step in range(FAN - 1):
            for way in range(2):
                @pl.when(sends(way, step))
                def _():
                    line_copy(buf, which, way, step).wait_send()

    def over_row(which, source, target, step):
        return copy(
            source, target, row_send.at[which, step - 1], row_recv.at[which, step - 1],
            device(sid, (r + step) % FAN),
        )

    def over_quad(which, source, target, step):
        return copy(
            source, target, quad_send.at[which, step - 1], quad_recv.at[which, step - 1],
            device(g * FAN + (q + step) % FAN, r),
        )

    def to_mate(source, target, number):
        return copy(source, target, pair_send.at[number], pair_recv.at[number], device(sid, mate))

    def to_partner(source, target, number):
        return copy(
            source, target, pair_send.at[number], pair_recv.at[number], device(sid, FAN - 1 - r)
        )

    def over_wide(source, target, step):
        return copy(
            source, target, wide_send.at[step - 1], wide_recv.at[step - 1],
            device((sid + step) % wide, r),
        )

    def over_tops(source, target, step):
        return copy(
            source, target, tops_send.at[step - 1], tops_recv.at[step - 1],
            device((g + step) % groups * FAN + q, r),
        )

    barrier = pltpu.get_barrier_semaphore()
    for step in range(1, FAN):
        pl.semaphore_signal(
            barrier, inc=1, device_id=device(sid, (r + step) % FAN),
            device_id_type=pl.DeviceIdType.MESH,
        )
    for step in range(1, wide):
        pl.semaphore_signal(
            barrier, inc=1, device_id=device((sid + step) % wide, r),
            device_id_type=pl.DeviceIdType.MESH,
        )
    pl.semaphore_wait(barrier, FAN - 1 + wide - 1)

    proj_end = to_mate(proj_all.at[r], proj_all.at[r], 0)
    proj_from = to_mate(proj_all.at[mate], proj_all.at[mate], 0)
    couple_end = [
        to_mate(couple_one.at[pl.ds(i * part_rows, part_rows)],
                couple_ward.at[pl.ds(i * part_rows, part_rows)], 1 + i)
        for i in range(FAN)
    ]
    trans_end = to_mate(trans_one_all.at[r], trans_one_all.at[r], 5)
    trans_from = to_mate(trans_one_all.at[mate], trans_one_all.at[mate], 5)
    proj_over = to_partner(proj_all.at[r], proj_all.at[r], 6)
    proj_pass = to_partner(proj_all.at[mate], proj_all.at[mate], 7)
    trans_over = to_partner(trans_one_all.at[r], trans_one_all.at[r], 8)
    trans_pass = to_partner(trans_one_all.at[mate], trans_one_all.at[mate], 9)
    reduce_over = to_partner(
        reduce_part.at[pl.ds((1 - r // 2) * 2, 2)], reduce_in, 10
    )
    reduce_ward = to_mate(ward_part, stack_two.at[q], 11)
    solve_back = to_mate(solve_ward, solve_one, 12)
    gain_back = to_mate(gain_ward, gain_one, 13)

    two_end = to_mate(couple_two_all.at[r], couple_two_all.at[r], 14)
    two_from = to_mate(couple_two_all.at[mate], couple_two_all.at[mate], 14)
    two_over = to_partner(couple_two_all.at[r], couple_two_all.at[r], 15)
    two_pass = to_partner(couple_two_all.at[mate], couple_two_all.at[mate], 16)
    across, beyond = FAN - 1 - r, FAN - 1 - mate
    two_own = to_mate(couple_two_all.at[r], couple_two_all.at[r], 17)
    two_across = to_mate(couple_two_all.at[across], couple_two_all.at[across], 18)
    two_beyond = to_mate(couple_two_all.at[beyond], couple_two_all.at[beyond], 19)

    inverse_load = pltpu.make_async_copy(inverse_hbm, inverse, local_sem.at[0])
    inverse_load.start()
    width = couple_two.shape[1]
    couple_two_all[r, :, :width] = couple_two[...]
    couple_two_all[r, :, width:] = transfer_two[...]
    trans_one_all[r] = transfer_one[...]
    top_rows[r, g] = couple_top[pl.ds(pl.multiple_of(g * slice_rows, slice_rows), slice_rows), :]

    @pl.when(outer)
    def _():
        two_end.start()
        trans_end.start()
        couple_end[0].start()

    @pl.when(inner)
    def _():
        two_over.start()
        two_own.start()
        trans_over.start()

    tops = []
    for s in range(1, groups):
        other = (g + s) % groups
        tops.append(
            over_tops(
                couple_top.at[pl.ds(pl.multiple_of(other * slice_rows, slice_rows), slice_rows)],
                top_rows.at[r, g],
                s,
            )
        )
        tops[-1].start()

    lab_high[...], lab_low[...] = split(labels[...])
    position = jnp.broadcast_to(order[...].astype(F32), (128, leaf)).T
    column[...] = position.astype(jnp.int32)
    rhs_high, rhs_low = placed_high, placed_low = sol_high.at[0], sol_low.at[0]
    sol_h, sol_l = sol_high.at[1], sol_low.at[1]
    tiles = leaf // tile

    def rows_of(step):
        return pl.ds(pl.multiple_of(step * tile, tile), tile)

    @pl.loop(0, tiles)
    def _(step):
        rows = rows_of(step)
        hot = column[rows, 0:1] == lax.broadcasted_iota(jnp.int32, (tile, leaf), 1)
        hot = hot.astype(F32).astype(BF16)
        rhs_high[rows, :] = dot(hot, lab_high[...]).astype(BF16)
        rhs_low[rows, :] = dot(hot, lab_low[...]).astype(BF16)

    inverse_load.wait()

    @pl.loop(0, tiles)
    def _(step):
        rows = rows_of(step)
        value = dot3(split(inverse[rows, :]), (rhs_high[...], rhs_low[...]))
        sol_h[rows, :], sol_l[rows, :] = split(value)

    @pl.when(inner)
    def _():
        two_from.wait_recv()
        two_pass.start()

    proj_all[r] = dot3(split(basis[...].T), (sol_h[...], sol_l[...]))

    @pl.when(outer)
    def _():
        proj_end.start()

    @pl.when(inner)
    def _():
        proj_over.start()

    basis_parts = split(basis[...])
    lab_high[:, :rank], lab_low[:, :rank] = basis_parts

    @pl.loop(0, tiles)
    def _(step):
        rows = rows_of(step)
        value = dot3(split(inverse[rows, :]), (lab_high[:, :rank], lab_low[:, :rank]))
        rhs_high[rows, :rank], rhs_low[rows, :rank] = split(value)

    @pl.when(outer)
    def _():
        proj_end.wait_send()
        for c in couple_end[1:]:
            c.start()

    @pl.when(inner)
    def _():
        two_over.wait_recv()
        two_across.start()
        proj_from.wait_recv()
        proj_pass.start()

    def hot_rows(step):
        hot = (lax.broadcasted_iota(jnp.int32, (tile, leaf), 0) + step * tile) == order[...]
        return hot.astype(F32).astype(BF16)

    @pl.loop(0, tiles)
    def _(step):
        rows = rows_of(step)
        hot = hot_rows(step)
        placed_out[rows, :] = dot(hot, sol_h[...]) + dot(hot, sol_l[...])

    placed_store = pltpu.make_async_copy(placed_out, placed_hbm, local_sem.at[1])
    placed_store.start()

    for c in tops:
        c.wait_recv()
    row_top = [over_row(0, top_rows.at[r], top_rows.at[r], s) for s in range(1, FAN)]

    @pl.when(inner)
    def _():
        two_pass.wait_recv()
        two_beyond.start()
        proj_over.wait_recv()
        proj_pass.wait_recv()

    for c in row_top:
        c.start()

    @pl.when(outer)
    def _():
        two_own.wait_recv()
        two_across.wait_recv()
        two_beyond.wait_recv()

    trans_two_all[q] = couple_two_all[:, :, width:]
    quad_two = [
        over_quad(0, trans_two_all.at[q], trans_two_all.at[q], s) for s in range(1, FAN)
    ]
    for c in quad_two:
        c.start()

    @pl.when(inner)
    def _():
        stack_one = split(flat(proj_all[...]))
        solve_one[...] = dot3(split(couple_one[...]), stack_one)
        reduced = matmul(transfer_one[...].T, solve_one[...])
        for c in couple_end:
            c.wait_recv()
        trans_from.wait_recv()
        solve_ward[...] = dot3(split(couple_ward[...]), stack_one)
        reduced = reduced + matmul(trans_one_all[mate].T, solve_ward[...])
        for part in range(FAN):
            reduce_part[part] = reduced[:, part * part_cols : (part + 1) * part_cols]
        reduce_over.start()
        reduce_over.wait_recv()
        ward_part[...] = reduce_part[mate] + reduce_in[mate % 2]
        reduce_ward.start()
        stack_two[q] = reduce_part[r] + reduce_in[r % 2]

    @pl.when(outer)
    def _():
        reduce_ward.wait_recv()

    quad_stack = [over_quad(1, stack_two.at[q], stack_two.at[q], s) for s in range(1, FAN)]
    for c in quad_stack:
        c.start()

    @pl.when(inner)
    def _():
        trans_pass.start()
        solve_back.start()

    @pl.loop(0, tiles)
    def _(step):
        rows = rows_of(step)
        hot = hot_rows(step)
        spread_out[rows, :] = dot(hot, rhs_high[:, :rank]) + dot(hot, rhs_low[:, :rank])

    spread_store = pltpu.make_async_copy(spread_out, spread_hbm, local_sem.at[2])
    spread_store.start()

    for c in row_top:
        c.wait_recv()

    couple = split(flat(couple_two_all[:, :, :width]))
    for c in quad_two:
        c.wait_recv()
    gain_two = split(dot3(couple, split(flat(trans_two_all[...]))))
    own_two = flat(trans_two_all[q]).T
    for c in quad_stack:
        c.wait_recv()
    solve_two = dot3(couple, split(flat(stack_two[...])))
    top_part[...] = matmul(own_two, solve_two).reshape(FAN, part_rows, part_cols)
    quad_reduce = [
        over_quad(2, top_part.at[(q + s) % FAN], top_in.at[s - 1], s) for s in range(1, FAN)
    ]
    for c in quad_reduce:
        c.start()
    for c in quad_reduce:
        c.wait_recv()
    top_all[sid] = top_part[q] + top_in[0] + (top_in[1] + top_in[2])
    wide_top = [over_wide(top_all.at[sid], top_all.at[sid], s) for s in range(1, wide)]
    for c in wide_top:
        c.start()
    for c in wide_top:
        c.wait_recv()
    total = jnp.zeros((part_rows, part_cols), F32)
    for other in range(groups):
        total = total + matmul(
            flat(top_rows[:, other]), flat(top_all[other * FAN : (other + 1) * FAN])
        )
    block_two[q] = total
    quad_block = [over_quad(3, block_two.at[q], block_two.at[q], s) for s in range(1, FAN)]
    for c in quad_block:
        c.start()
    for c in quad_block:
        c.wait_recv()
    fixed_two_all[r] = solve_two - dot3(gain_two, split(flat(block_two[...])))
    line_start(fixed_two_all, 0, 0)

    @pl.when(inner)
    def _():
        trans_over.wait_recv()
        trans_pass.wait_recv()
        trans_full = split(flat(trans_one_all[...]))
        gain_ward[...] = dot3(split(couple_ward[...]), trans_full)
        gain_back.start()
        gain_one[...] = dot3(split(couple_one[...]), trans_full)

    line_wait(fixed_two_all, 0, 0)
    line_start(fixed_two_all, 0, 1)
    line_wait(fixed_two_all, 0, 1)
    line_start(fixed_two_all, 0, 2)
    line_wait(fixed_two_all, 0, 2)

    @pl.when(outer)
    def _():
        solve_back.wait_recv()
        gain_back.wait_recv()

    gain = split(gain_one[...])
    for part in range(FAN):
        here = slice(part * part_cols, (part + 1) * part_cols)
        block_out[:, here] = solve_one[:, here] - dot3(gain, split(fixed_two_all[part]))

    for which, buf in enumerate((fixed_two_all,)):
        line_finish(buf, which)

    @pl.when(outer)
    def _():
        for c in couple_end:
            c.wait_send()
        trans_end.wait_send()
        two_end.wait_send()

    @pl.when(inner)
    def _():
        for c in (
            proj_over, proj_pass, trans_over, trans_pass, reduce_over, reduce_ward,
            solve_back, gain_back, two_over, two_pass, two_own, two_across, two_beyond,
        ):
            c.wait_send()

    for c in tops + row_top + quad_two + quad_stack + quad_reduce + wide_top + quad_block:
        c.wait_send()
    placed_store.wait()
    spread_store.wait()


def per_device(
    depth,
    groups,
    labels,
    point_order,
    leaf_inverse,
    leaf_basis,
    couple_one,
    transfer_one,
    couple_two,
    transfer_two,
    couple_top,
):
    leaf, cols = labels.shape
    rank = leaf_basis.shape[1]
    part_cols = cols // FAN
    part_rows = rank // FAN
    slice_rows = couple_top.shape[0] // groups
    wide = FAN * groups
    vmem = pl.BlockSpec(memory_space=pltpu.VMEM)
    far = pl.BlockSpec(memory_space=pl.ANY)
    dma = pltpu.SemaphoreType.DMA
    args = (
        labels, point_order, leaf_inverse, leaf_basis, couple_one, transfer_one,
        couple_two, transfer_two, couple_top,
    )
    placed, spread, block = pl.pallas_call(
        functools.partial(kernel, depth, groups, leaf // TILES),
        out_shape=(
            jax.ShapeDtypeStruct((leaf, cols), F32),
            jax.ShapeDtypeStruct((leaf, rank), F32),
            jax.ShapeDtypeStruct((rank, cols), F32),
        ),
        in_specs=[vmem, vmem, far] + [vmem] * (len(args) - 3),
        out_specs=(far, far, vmem),
        scratch_shapes=[
            pltpu.VMEM((leaf, cols), F32),
            pltpu.VMEM((leaf, rank), F32),
            pltpu.VMEM((leaf, leaf), F32),
            pltpu.VMEM((leaf, cols), BF16),
            pltpu.VMEM((leaf, cols), BF16),
            pltpu.VMEM((2, leaf, cols), BF16),
            pltpu.VMEM((2, leaf, cols), BF16),
            pltpu.VMEM((leaf, 128), jnp.int32),
            pltpu.VMEM((FAN, rank, cols), F32),
            pltpu.VMEM((FAN, *transfer_one.shape), F32),
            pltpu.VMEM((FAN, couple_two.shape[0], couple_two.shape[1] + rank), F32),
            pltpu.VMEM((FAN, rank, part_cols), F32),
            pltpu.VMEM((FAN, rank, part_cols), F32),
            pltpu.VMEM((2, rank, part_cols), F32),
            pltpu.VMEM((FAN, rank, part_cols), F32),
            pltpu.VMEM((FAN, FAN, *transfer_two.shape), F32),
            pltpu.VMEM((FAN, part_rows, part_cols), F32),
            pltpu.VMEM((FAN - 1, part_rows, part_cols), F32),
            pltpu.VMEM((wide, part_rows, part_cols), F32),
            pltpu.VMEM((FAN, part_rows, part_cols), F32),
            pltpu.VMEM((FAN, groups, slice_rows, rank), F32),
            pltpu.VMEM((rank, cols), F32),
            pltpu.VMEM((rank, rank), F32),
            pltpu.VMEM(couple_one.shape, F32),
            pltpu.VMEM((rank, cols), F32),
            pltpu.VMEM((rank, rank), F32),
            pltpu.VMEM((rank, part_cols), F32),
            dma((20,)),
            dma((20,)),
            dma((3,)),
            dma((1, 2, FAN - 1)),
            dma((1, 2, FAN - 1)),
            dma((1, FAN - 1)),
            dma((1, FAN - 1)),
            dma((4, FAN - 1)),
            dma((4, FAN - 1)),
            dma((wide - 1,)),
            dma((wide - 1,)),
            dma((max(groups - 1, 1),)),
            dma((max(groups - 1, 1),)),
        ],
        compiler_params=pltpu.CompilerParams(
            collective_id=0, has_side_effects=True, vmem_limit_bytes=56 * 1024 * 1024
        ),
    )(*args)
    return placed - jnp.dot(spread, block, precision=lax.Precision.HIGH)


def solution(mesh):
    depth = mesh.shape["gy"]
    groups = mesh.shape["gx"] * depth // (FAN * FAN)
    spec = P(("gx", "gy"), None)
    return jax.shard_map(
        functools.partial(per_device, depth, groups),
        mesh=mesh,
        in_specs=(spec,) * 9,
        out_specs=spec,
        check_vma=False,
    )
```

```python
import functools

import jax
import jax.numpy as jnp
from jax import lax
from jax.experimental import pallas as pl
from jax.experimental.pallas import tpu as pltpu
from jax.sharding import PartitionSpec as P

F32 = jnp.float32
BF16 = jnp.bfloat16
FAN = 4
TILES = 2


def split(x):
    high = x.astype(BF16)
    return high, (x - high.astype(F32)).astype(BF16)


def dot(left, right):
    return jnp.dot(left, right, preferred_element_type=F32)


def dot3(left, right):
    return dot(left[0], right[0]) + (dot(left[0], right[1]) + dot(left[1], right[0]))


def matmul(left, right):
    return dot3(split(left), split(right))


def flat(block):
    return block.reshape(-1, block.shape[-1])


def kernel(
    depth,
    groups,
    tile,
    labels,
    order,
    inverse_hbm,
    basis,
    couple_one,
    transfer_one,
    couple_two,
    transfer_two,
    couple_top,
    placed_hbm,
    spread_high_hbm,
    spread_low_hbm,
    block_high,
    block_low,
    placed_out,
    spread_high,
    spread_low,
    inverse,
    lab_high,
    lab_low,
    sol_high,
    sol_low,
    column,
    proj_all,
    trans_one_all,
    couple_two_all,
    fixed_two_all,
    reduce_part,
    reduce_in,
    stack_two,
    trans_two_all,
    top_part,
    top_in,
    top_all,
    top_rows,
    solve_one,
    gain_one,
    couple_ward,
    solve_ward,
    gain_ward,
    ward_part,
    pair_send,
    pair_recv,
    local_sem,
    line_send,
    line_recv,
    row_send,
    row_recv,
    quad_send,
    quad_recv,
    wide_send,
    wide_recv,
    tops_send,
    tops_recv,
):
    index = lax.axis_index("gx") * depth + lax.axis_index("gy")
    r = index % FAN
    sid = index // FAN
    q = sid % FAN
    g = sid // FAN
    wide = FAN * groups
    leaf, cols = labels.shape
    rank = basis.shape[1]
    part_cols = cols // FAN
    part_rows = rank // FAN
    slice_rows = couple_top.shape[0] // groups

    mate = r + 1 - 2 * (r % 2)
    inner = jnp.logical_and(r > 0, r < FAN - 1)
    outer = jnp.logical_not(inner)

    def device(sid_of, r_of):
        place = sid_of * FAN + r_of
        return (place // depth, place % depth)

    def copy(source, target, send, recv, where):
        return pltpu.make_async_remote_copy(
            src_ref=source,
            dst_ref=target,
            send_sem=send,
            recv_sem=recv,
            device_id=where,
            device_id_type=pl.DeviceIdType.MESH,
        )

    def line_copy(buf, which, way, step):
        slot = r - step if way == 0 else r + step
        to = r + 1 if way == 0 else r - 1
        slot = jnp.clip(slot, 0, FAN - 1)
        to = jnp.clip(to, 0, FAN - 1)
        return copy(
            buf.at[slot],
            buf.at[slot],
            line_send.at[which, way, step],
            line_recv.at[which, way, step],
            device(sid, to),
        )

    def sends(way, step):
        if way == 0:
            return jnp.logical_and(r >= step, r < FAN - 1)
        return jnp.logical_and(r + step <= FAN - 1, r > 0)

    def receives(way, step):
        if way == 0:
            return r - 1 - step >= 0
        return r + 1 + step <= FAN - 1

    def line_start(buf, which, step):
        for way in range(2):
            @pl.when(sends(way, step))
            def _():
                line_copy(buf, which, way, step).start()

    def line_wait(buf, which, step):
        for way in range(2):
            @pl.when(receives(way, step))
            def _():
                slot = r - 1 - step if way == 0 else r + 1 + step
                slot = jnp.clip(slot, 0, FAN - 1)
                copy(
                    buf.at[slot],
                    buf.at[slot],
                    line_send.at[which, way, step],
                    line_recv.at[which, way, step],
                    device(sid, (r + 1) % FAN),
                ).wait_recv()

    def line_finish(buf, which):
        for step in range(FAN - 1):
            for way in range(2):
                @pl.when(sends(way, step))
                def _():
                    line_copy(buf, which, way, step).wait_send()

    def over_row(which, source, target, step):
        return copy(
            source, target, row_send.at[which, step - 1], row_recv.at[which, step - 1],
            device(sid, (r + step) % FAN),
        )

    def over_quad(which, source, target, step):
        return copy(
            source, target, quad_send.at[which, step - 1], quad_recv.at[which, step - 1],
            device(g * FAN + (q + step) % FAN, r),
        )

    def to_mate(source, target, number):
        return copy(source, target, pair_send.at[number], pair_recv.at[number], device(sid, mate))

    def to_partner(source, target, number):
        return copy(
            source, target, pair_send.at[number], pair_recv.at[number], device(sid, FAN - 1 - r)
        )

    def over_wide(source, target, step):
        return copy(
            source, target, wide_send.at[step - 1], wide_recv.at[step - 1],
            device((sid + step) % wide, r),
        )

    def over_tops(source, target, step):
        return copy(
            source, target, tops_send.at[step - 1], tops_recv.at[step - 1],
            device((g + step) % groups * FAN + q, r),
        )

    barrier = pltpu.get_barrier_semaphore()
    for step in range(1, FAN):
        pl.semaphore_signal(
            barrier, inc=1, device_id=device(sid, (r + step) % FAN),
            device_id_type=pl.DeviceIdType.MESH,
        )
    for step in range(1, wide):
        pl.semaphore_signal(
            barrier, inc=1, device_id=device((sid + step) % wide, r),
            device_id_type=pl.DeviceIdType.MESH,
        )
    pl.semaphore_wait(barrier, FAN - 1 + wide - 1)

    proj_end = to_mate(proj_all.at[r], proj_all.at[r], 0)
    proj_from = to_mate(proj_all.at[mate], proj_all.at[mate], 0)
    couple_end = [
        to_mate(couple_one.at[pl.ds(i * part_rows, part_rows)],
                couple_ward.at[pl.ds(i * part_rows, part_rows)], 1 + i)
        for i in range(FAN)
    ]
    trans_end = to_mate(trans_one_all.at[r], trans_one_all.at[r], 5)
    trans_from = to_mate(trans_one_all.at[mate], trans_one_all.at[mate], 5)
    proj_over = to_partner(proj_all.at[r], proj_all.at[r], 6)
    proj_pass = to_partner(proj_all.at[mate], proj_all.at[mate], 7)
    trans_over = to_partner(trans_one_all.at[r], trans_one_all.at[r], 8)
    trans_pass = to_partner(trans_one_all.at[mate], trans_one_all.at[mate], 9)
    reduce_over = to_partner(
        reduce_part.at[pl.ds((1 - r // 2) * 2, 2)], reduce_in, 10
    )
    reduce_ward = to_mate(ward_part, stack_two.at[q], 11)
    solve_back = to_mate(solve_ward, solve_one, 12)
    gain_back = to_mate(gain_ward, gain_one, 13)

    two_end = to_mate(couple_two_all.at[r], couple_two_all.at[r], 14)
    two_from = to_mate(couple_two_all.at[mate], couple_two_all.at[mate], 14)
    two_over = to_partner(couple_two_all.at[r], couple_two_all.at[r], 15)
    two_pass = to_partner(couple_two_all.at[mate], couple_two_all.at[mate], 16)
    across, beyond = FAN - 1 - r, FAN - 1 - mate
    two_own = to_mate(couple_two_all.at[r], couple_two_all.at[r], 17)
    two_across = to_mate(couple_two_all.at[across], couple_two_all.at[across], 18)
    two_beyond = to_mate(couple_two_all.at[beyond], couple_two_all.at[beyond], 19)

    inverse_load = pltpu.make_async_copy(inverse_hbm, inverse, local_sem.at[0])
    inverse_load.start()
    width = couple_two.shape[1]
    couple_two_all[r, :, :width] = couple_two[...]
    couple_two_all[r, :, width:] = transfer_two[...]
    trans_one_all[r] = transfer_one[...]
    top_rows[q, r, g] = couple_top[pl.ds(pl.multiple_of(g * slice_rows, slice_rows), slice_rows), :]

    @pl.when(outer)
    def _():
        two_end.start()
        trans_end.start()
        couple_end[0].start()

    @pl.when(inner)
    def _():
        two_over.start()
        two_own.start()
        trans_over.start()

    tops = []
    for s in range(1, groups):
        other = (g + s) % groups
        tops.append(
            over_tops(
                couple_top.at[pl.ds(pl.multiple_of(other * slice_rows, slice_rows), slice_rows)],
                top_rows.at[q, r, g],
                s,
            )
        )
        tops[-1].start()

    lab_high[...], lab_low[...] = split(labels[...])
    position = jnp.broadcast_to(order[...].astype(F32), (128, leaf)).T
    column[...] = position.astype(jnp.int32)
    rhs_high, rhs_low = placed_high, placed_low = sol_high.at[0], sol_low.at[0]
    sol_h, sol_l = sol_high.at[1], sol_low.at[1]
    tiles = leaf // tile

    def rows_of(step):
        return pl.ds(pl.multiple_of(step * tile, tile), tile)

    @pl.loop(0, tiles)
    def _(step):
        rows = rows_of(step)
        hot = column[rows, 0:1] == lax.broadcasted_iota(jnp.int32, (tile, leaf), 1)
        hot = hot.astype(F32).astype(BF16)
        rhs_high[rows, :] = dot(hot, lab_high[...]).astype(BF16)
        rhs_low[rows, :] = dot(hot, lab_low[...]).astype(BF16)

    inverse_load.wait()

    @pl.loop(0, tiles)
    def _(step):
        rows = rows_of(step)
        value = dot3(split(inverse[rows, :]), (rhs_high[...], rhs_low[...]))
        sol_h[rows, :], sol_l[rows, :] = split(value)

    @pl.when(inner)
    def _():
        two_from.wait_recv()
        two_pass.start()

    proj_all[r] = dot3(split(basis[...].T), (sol_h[...], sol_l[...]))

    @pl.when(outer)
    def _():
        proj_end.start()

    @pl.when(inner)
    def _():
        proj_over.start()

    basis_parts = split(basis[...])
    lab_high[:, :rank], lab_low[:, :rank] = basis_parts

    @pl.loop(0, tiles)
    def _(step):
        rows = rows_of(step)
        value = dot3(split(inverse[rows, :]), (lab_high[:, :rank], lab_low[:, :rank]))
        rhs_high[rows, :rank], rhs_low[rows, :rank] = split(value)

    @pl.when(outer)
    def _():
        proj_end.wait_send()
        for c in couple_end[1:]:
            c.start()

    @pl.when(inner)
    def _():
        two_over.wait_recv()
        two_across.start()
        proj_from.wait_recv()
        proj_pass.start()

    def hot_rows(step):
        hot = (lax.broadcasted_iota(jnp.int32, (tile, leaf), 0) + step * tile) == order[...]
        return hot.astype(F32).astype(BF16)

    @pl.loop(0, tiles)
    def _(step):
        rows = rows_of(step)
        hot = hot_rows(step)
        placed_out[rows, :] = dot(hot, sol_h[...]) + dot(hot, sol_l[...])

    placed_store = pltpu.make_async_copy(placed_out, placed_hbm, local_sem.at[1])
    placed_store.start()

    for c in tops:
        c.wait_recv()
    row_top = [over_row(0, top_rows.at[q, r], top_rows.at[q, r], s) for s in range(1, FAN)]
    for c in row_top:
        c.start()

    @pl.when(inner)
    def _():
        two_pass.wait_recv()
        two_beyond.start()
        proj_over.wait_recv()
        proj_pass.wait_recv()

    @pl.when(outer)
    def _():
        two_own.wait_recv()
        two_across.wait_recv()
        two_beyond.wait_recv()

    trans_two_all[q] = couple_two_all[:, :, width:]
    quad_two = [
        over_quad(0, trans_two_all.at[q], trans_two_all.at[q], s) for s in range(1, FAN)
    ]
    for c in quad_two:
        c.start()

    for c in row_top:
        c.wait_recv()
    quad_top = [over_quad(3, top_rows.at[q], top_rows.at[q], s) for s in range(1, FAN)]
    for c in quad_top:
        c.start()

    @pl.when(inner)
    def _():
        stack_one = split(flat(proj_all[...]))
        solve_one[...] = dot3(split(couple_one[...]), stack_one)
        reduced = matmul(transfer_one[...].T, solve_one[...])
        for c in couple_end:
            c.wait_recv()
        trans_from.wait_recv()
        solve_ward[...] = dot3(split(couple_ward[...]), stack_one)
        reduced = reduced + matmul(trans_one_all[mate].T, solve_ward[...])
        for part in range(FAN):
            reduce_part[part] = reduced[:, part * part_cols : (part + 1) * part_cols]
        reduce_over.start()
        reduce_over.wait_recv()
        ward_part[...] = reduce_part[mate] + reduce_in[mate % 2]
        reduce_ward.start()
        stack_two[q] = reduce_part[r] + reduce_in[r % 2]

    @pl.when(outer)
    def _():
        reduce_ward.wait_recv()

    quad_stack = [over_quad(1, stack_two.at[q], stack_two.at[q], s) for s in range(1, FAN)]
    for c in quad_stack:
        c.start()

    @pl.when(inner)
    def _():
        trans_pass.start()
        solve_back.start()

    @pl.loop(0, tiles)
    def _(step):
        rows = rows_of(step)
        hot = hot_rows(step)
        spread_high[rows, :] = dot(hot, rhs_high[:, :rank]).astype(BF16)
        spread_low[rows, :] = dot(hot, rhs_low[:, :rank]).astype(BF16)

    spread_store = [
        pltpu.make_async_copy(spread_high, spread_high_hbm, local_sem.at[2]),
        pltpu.make_async_copy(spread_low, spread_low_hbm, local_sem.at[3]),
    ]
    for c in spread_store:
        c.start()


    couple = split(flat(couple_two_all[:, :, :width]))
    for c in quad_two:
        c.wait_recv()
    gain_two = split(dot3(couple, split(flat(trans_two_all[...]))))
    own_two = flat(trans_two_all[q]).T
    for c in quad_stack:
        c.wait_recv()
    solve_two = dot3(couple, split(flat(stack_two[...])))
    top_part[...] = matmul(own_two, solve_two).reshape(FAN, part_rows, part_cols)
    quad_reduce = [
        over_quad(2, top_part.at[(q + s) % FAN], top_in.at[s - 1], s) for s in range(1, FAN)
    ]
    for c in quad_reduce:
        c.start()
    for c in quad_reduce:
        c.wait_recv()
    top_all[sid] = top_part[q] + top_in[0] + (top_in[1] + top_in[2])
    wide_top = [over_wide(top_all.at[sid], top_all.at[sid], s) for s in range(1, wide)]
    for c in wide_top:
        c.start()
    for c in wide_top:
        c.wait_recv()
    for c in quad_top:
        c.wait_recv()
    total = jnp.zeros((rank, part_cols), F32)
    for other in range(groups):
        total = total + matmul(
            flat(top_rows[:, :, other]), flat(top_all[other * FAN : (other + 1) * FAN])
        )
    fixed_two_all[r] = solve_two - dot3(gain_two, split(total))
    line_start(fixed_two_all, 0, 0)

    @pl.when(inner)
    def _():
        trans_over.wait_recv()
        trans_pass.wait_recv()
        trans_full = split(flat(trans_one_all[...]))
        gain_ward[...] = dot3(split(couple_ward[...]), trans_full)
        gain_back.start()
        gain_one[...] = dot3(split(couple_one[...]), trans_full)

    line_wait(fixed_two_all, 0, 0)
    line_start(fixed_two_all, 0, 1)
    line_wait(fixed_two_all, 0, 1)
    line_start(fixed_two_all, 0, 2)
    line_wait(fixed_two_all, 0, 2)

    @pl.when(outer)
    def _():
        solve_back.wait_recv()
        gain_back.wait_recv()

    gain = split(gain_one[...])
    for part in range(FAN):
        here = slice(part * part_cols, (part + 1) * part_cols)
        value = solve_one[:, here] - dot3(gain, split(fixed_two_all[part]))
        block_high[:, here], block_low[:, here] = split(value)

    for which, buf in enumerate((fixed_two_all,)):
        line_finish(buf, which)

    @pl.when(outer)
    def _():
        for c in couple_end:
            c.wait_send()
        trans_end.wait_send()
        two_end.wait_send()

    @pl.when(inner)
    def _():
        for c in (
            proj_over, proj_pass, trans_over, trans_pass, reduce_over, reduce_ward,
            solve_back, gain_back, two_over, two_pass, two_own, two_across, two_beyond,
        ):
            c.wait_send()

    for c in tops + row_top + quad_two + quad_stack + quad_reduce + wide_top + quad_top:
        c.wait_send()
    placed_store.wait()
    for c in spread_store:
        c.wait()


def last(placed, spread_high, spread_low, block_high, block_low, out):
    out[...] = placed[...] - dot3(
        (spread_high[...], spread_low[...]), (block_high[...], block_low[...])
    )


def per_device(
    depth,
    groups,
    labels,
    point_order,
    leaf_inverse,
    leaf_basis,
    couple_one,
    transfer_one,
    couple_two,
    transfer_two,
    couple_top,
):
    leaf, cols = labels.shape
    rank = leaf_basis.shape[1]
    part_cols = cols // FAN
    part_rows = rank // FAN
    slice_rows = couple_top.shape[0] // groups
    wide = FAN * groups
    vmem = pl.BlockSpec(memory_space=pltpu.VMEM)
    far = pl.BlockSpec(memory_space=pl.ANY)
    dma = pltpu.SemaphoreType.DMA
    args = (
        labels, point_order, leaf_inverse, leaf_basis, couple_one, transfer_one,
        couple_two, transfer_two, couple_top,
    )
    placed, *parts = pl.pallas_call(
        functools.partial(kernel, depth, groups, leaf // TILES),
        out_shape=(
            jax.ShapeDtypeStruct((leaf, cols), F32),
            jax.ShapeDtypeStruct((leaf, rank), BF16),
            jax.ShapeDtypeStruct((leaf, rank), BF16),
            jax.ShapeDtypeStruct((rank, cols), BF16),
            jax.ShapeDtypeStruct((rank, cols), BF16),
        ),
        in_specs=[vmem, vmem, far] + [vmem] * (len(args) - 3),
        out_specs=(far, far, far, vmem, vmem),
        scratch_shapes=[
            pltpu.VMEM((leaf, cols), F32),
            pltpu.VMEM((leaf, rank), BF16),
            pltpu.VMEM((leaf, rank), BF16),
            pltpu.VMEM((leaf, leaf), F32),
            pltpu.VMEM((leaf, cols), BF16),
            pltpu.VMEM((leaf, cols), BF16),
            pltpu.VMEM((2, leaf, cols), BF16),
            pltpu.VMEM((2, leaf, cols), BF16),
            pltpu.VMEM((leaf, 128), jnp.int32),
            pltpu.VMEM((FAN, rank, cols), F32),
            pltpu.VMEM((FAN, *transfer_one.shape), F32),
            pltpu.VMEM((FAN, couple_two.shape[0], couple_two.shape[1] + rank), F32),
            pltpu.VMEM((FAN, rank, part_cols), F32),
            pltpu.VMEM((FAN, rank, part_cols), F32),
            pltpu.VMEM((2, rank, part_cols), F32),
            pltpu.VMEM((FAN, rank, part_cols), F32),
            pltpu.VMEM((FAN, FAN, *transfer_two.shape), F32),
            pltpu.VMEM((FAN, part_rows, part_cols), F32),
            pltpu.VMEM((FAN - 1, part_rows, part_cols), F32),
            pltpu.VMEM((wide, part_rows, part_cols), F32),
            pltpu.VMEM((FAN, FAN, groups, slice_rows, rank), F32),
            pltpu.VMEM((rank, cols), F32),
            pltpu.VMEM((rank, rank), F32),
            pltpu.VMEM(couple_one.shape, F32),
            pltpu.VMEM((rank, cols), F32),
            pltpu.VMEM((rank, rank), F32),
            pltpu.VMEM((rank, part_cols), F32),
            dma((20,)),
            dma((20,)),
            dma((4,)),
            dma((1, 2, FAN - 1)),
            dma((1, 2, FAN - 1)),
            dma((1, FAN - 1)),
            dma((1, FAN - 1)),
            dma((4, FAN - 1)),
            dma((4, FAN - 1)),
            dma((wide - 1,)),
            dma((wide - 1,)),
            dma((max(groups - 1, 1),)),
            dma((max(groups - 1, 1),)),
        ],
        compiler_params=pltpu.CompilerParams(
            collective_id=0, has_side_effects=True, vmem_limit_bytes=56 * 1024 * 1024
        ),
    )(*args)
    tile = leaf // 4
    spread_spec = pl.BlockSpec((tile, rank), lambda i: (i, 0))
    block_spec = pl.BlockSpec((rank, cols), lambda i: (0, 0))
    return pl.pallas_call(
        last,
        out_shape=jax.ShapeDtypeStruct((leaf, cols), F32),
        grid=(leaf // tile,),
        in_specs=[
            pl.BlockSpec((tile, cols), lambda i: (i, 0)),
            spread_spec, spread_spec, block_spec, block_spec,
        ],
        out_specs=pl.BlockSpec((tile, cols), lambda i: (i, 0)),
        compiler_params=pltpu.CompilerParams(vmem_limit_bytes=60 * 1024 * 1024),
    )(placed, *parts)


def solution(mesh):
    depth = mesh.shape["gy"]
    groups = mesh.shape["gx"] * depth // (FAN * FAN)
    spec = P(("gx", "gy"), None)
    return jax.shard_map(
        functools.partial(per_device, depth, groups),
        mesh=mesh,
        in_specs=(spec,) * 9,
        out_specs=spec,
        check_vma=False,
    )
```

```python
import functools

import jax
import jax.numpy as jnp
from jax import lax
from jax.experimental import pallas as pl
from jax.experimental.pallas import tpu as pltpu
from jax.sharding import PartitionSpec as P

F32 = jnp.float32
BF16 = jnp.bfloat16
FAN = 4
TILES = 2


def split(x):
    high = x.astype(BF16)
    return high, (x - high.astype(F32)).astype(BF16)


def dot(left, right):
    return jnp.dot(left, right, preferred_element_type=F32)


def dot3(left, right):
    return dot(left[0], right[0]) + (dot(left[0], right[1]) + dot(left[1], right[0]))


def matmul(left, right):
    return dot3(split(left), split(right))


def flat(block):
    return block.reshape(-1, block.shape[-1])


def kernel(
    depth,
    groups,
    tile,
    labels,
    order,
    inverse_hbm,
    basis,
    couple_one,
    transfer_one,
    couple_two,
    transfer_two,
    couple_top,
    placed_hbm,
    spread_high_hbm,
    spread_low_hbm,
    block_high,
    block_low,
    placed_out,
    spread_high,
    spread_low,
    inverse,
    lab_high,
    lab_low,
    sol_high,
    sol_low,
    column,
    proj_all,
    trans_one_all,
    couple_two_all,
    fixed_two_all,
    reduce_part,
    reduce_in,
    stack_two,
    trans_two_all,
    top_part,
    top_in,
    top_all,
    top_rows,
    solve_one,
    gain_one,
    couple_ward,
    solve_ward,
    gain_ward,
    ward_part,
    pair_send,
    pair_recv,
    local_sem,
    line_send,
    line_recv,
    row_send,
    row_recv,
    quad_send,
    quad_recv,
    wide_send,
    wide_recv,
    tops_send,
    tops_recv,
):
    index = lax.axis_index("gx") * depth + lax.axis_index("gy")
    r = index % FAN
    sid = index // FAN
    q = sid % FAN
    g = sid // FAN
    wide = FAN * groups
    leaf, cols = labels.shape
    rank = basis.shape[1]
    part_cols = cols // FAN
    part_rows = rank // FAN
    slice_rows = couple_top.shape[0] // groups

    mate = r + 1 - 2 * (r % 2)
    inner = jnp.logical_and(r > 0, r < FAN - 1)
    outer = jnp.logical_not(inner)

    def device(sid_of, r_of):
        place = sid_of * FAN + r_of
        return (place // depth, place % depth)

    def copy(source, target, send, recv, where):
        return pltpu.make_async_remote_copy(
            src_ref=source,
            dst_ref=target,
            send_sem=send,
            recv_sem=recv,
            device_id=where,
            device_id_type=pl.DeviceIdType.MESH,
        )

    def line_copy(buf, which, way, step):
        slot = r - step if way == 0 else r + step
        to = r + 1 if way == 0 else r - 1
        slot = jnp.clip(slot, 0, FAN - 1)
        to = jnp.clip(to, 0, FAN - 1)
        return copy(
            buf.at[slot],
            buf.at[slot],
            line_send.at[which, way, step],
            line_recv.at[which, way, step],
            device(sid, to),
        )

    def sends(way, step):
        if way == 0:
            return jnp.logical_and(r >= step, r < FAN - 1)
        return jnp.logical_and(r + step <= FAN - 1, r > 0)

    def receives(way, step):
        if way == 0:
            return r - 1 - step >= 0
        return r + 1 + step <= FAN - 1

    def line_start(buf, which, step):
        for way in range(2):
            @pl.when(sends(way, step))
            def _():
                line_copy(buf, which, way, step).start()

    def line_wait(buf, which, step):
        for way in range(2):
            @pl.when(receives(way, step))
            def _():
                slot = r - 1 - step if way == 0 else r + 1 + step
                slot = jnp.clip(slot, 0, FAN - 1)
                copy(
                    buf.at[slot],
                    buf.at[slot],
                    line_send.at[which, way, step],
                    line_recv.at[which, way, step],
                    device(sid, (r + 1) % FAN),
                ).wait_recv()

    def line_finish(buf, which):
        for step in range(FAN - 1):
            for way in range(2):
                @pl.when(sends(way, step))
                def _():
                    line_copy(buf, which, way, step).wait_send()

    def over_row(which, source, target, step):
        return copy(
            source, target, row_send.at[which, step - 1], row_recv.at[which, step - 1],
            device(sid, (r + step) % FAN),
        )

    def over_quad(which, source, target, step):
        return copy(
            source, target, quad_send.at[which, step - 1], quad_recv.at[which, step - 1],
            device(g * FAN + (q + step) % FAN, r),
        )

    def to_mate(source, target, number):
        return copy(source, target, pair_send.at[number], pair_recv.at[number], device(sid, mate))

    def to_partner(source, target, number):
        return copy(
            source, target, pair_send.at[number], pair_recv.at[number], device(sid, FAN - 1 - r)
        )

    def over_wide(source, target, step):
        return copy(
            source, target, wide_send.at[step - 1], wide_recv.at[step - 1],
            device((sid + step) % wide, r),
        )

    def over_tops(source, target, step):
        return copy(
            source, target, tops_send.at[step - 1], tops_recv.at[step - 1],
            device((g + step) % groups * FAN + q, r),
        )

    barrier = pltpu.get_barrier_semaphore()
    for step in range(1, FAN):
        pl.semaphore_signal(
            barrier, inc=1, device_id=device(sid, (r + step) % FAN),
            device_id_type=pl.DeviceIdType.MESH,
        )
    for step in range(1, wide):
        pl.semaphore_signal(
            barrier, inc=1, device_id=device((sid + step) % wide, r),
            device_id_type=pl.DeviceIdType.MESH,
        )
    pl.semaphore_wait(barrier, FAN - 1 + wide - 1)

    proj_end = to_mate(proj_all.at[r], proj_all.at[r], 0)
    proj_from = to_mate(proj_all.at[mate], proj_all.at[mate], 0)
    couple_end = [
        to_mate(couple_one.at[pl.ds(i * part_rows, part_rows)],
                couple_ward.at[pl.ds(i * part_rows, part_rows)], 1 + i)
        for i in range(FAN)
    ]
    trans_end = to_mate(trans_one_all.at[r], trans_one_all.at[r], 5)
    trans_from = to_mate(trans_one_all.at[mate], trans_one_all.at[mate], 5)
    proj_over = to_partner(proj_all.at[r], proj_all.at[r], 6)
    proj_pass = to_partner(proj_all.at[mate], proj_all.at[mate], 7)
    trans_over = to_partner(trans_one_all.at[r], trans_one_all.at[r], 8)
    trans_pass = to_partner(trans_one_all.at[mate], trans_one_all.at[mate], 9)
    reduce_over = to_partner(
        reduce_part.at[pl.ds((1 - r // 2) * 2, 2)], reduce_in, 10
    )
    reduce_ward = to_mate(ward_part, stack_two.at[q], 11)
    solve_back = to_mate(solve_ward, solve_one, 12)
    gain_back = to_mate(gain_ward, gain_one, 13)

    two_end = to_mate(couple_two_all.at[r], couple_two_all.at[r], 14)
    two_from = to_mate(couple_two_all.at[mate], couple_two_all.at[mate], 14)
    two_over = to_partner(couple_two_all.at[r], couple_two_all.at[r], 15)
    two_pass = to_partner(couple_two_all.at[mate], couple_two_all.at[mate], 16)
    across, beyond = FAN - 1 - r, FAN - 1 - mate
    two_own = to_mate(couple_two_all.at[r], couple_two_all.at[r], 17)
    two_across = to_mate(couple_two_all.at[across], couple_two_all.at[across], 18)
    two_beyond = to_mate(couple_two_all.at[beyond], couple_two_all.at[beyond], 19)

    inverse_load = pltpu.make_async_copy(inverse_hbm, inverse, local_sem.at[0])
    inverse_load.start()
    width = couple_two.shape[1]
    couple_two_all[r, :, :width] = couple_two[...]
    couple_two_all[r, :, width:] = transfer_two[...]
    trans_one_all[r] = transfer_one[...]
    top_rows[q, r, g] = couple_top[pl.ds(pl.multiple_of(g * slice_rows, slice_rows), slice_rows), :]

    @pl.when(outer)
    def _():
        two_end.start()
        trans_end.start()
        couple_end[0].start()

    @pl.when(inner)
    def _():
        two_over.start()
        two_own.start()
        trans_over.start()

    tops = []
    for s in range(1, groups):
        other = (g + s) % groups
        tops.append(
            over_tops(
                couple_top.at[pl.ds(pl.multiple_of(other * slice_rows, slice_rows), slice_rows)],
                top_rows.at[q, r, g],
                s,
            )
        )
        tops[-1].start()

    lab_high[...], lab_low[...] = split(labels[...])
    position = jnp.broadcast_to(order[...].astype(F32), (128, leaf)).T
    column[...] = position.astype(jnp.int32)
    rhs_high, rhs_low = placed_high, placed_low = sol_high.at[0], sol_low.at[0]
    sol_h, sol_l = sol_high.at[1], sol_low.at[1]
    tiles = leaf // tile

    def rows_of(step):
        return pl.ds(pl.multiple_of(step * tile, tile), tile)

    @pl.loop(0, tiles)
    def _(step):
        rows = rows_of(step)
        hot = column[rows, 0:1] == lax.broadcasted_iota(jnp.int32, (tile, leaf), 1)
        hot = hot.astype(F32).astype(BF16)
        rhs_high[rows, :] = dot(hot, lab_high[...]).astype(BF16)
        rhs_low[rows, :] = dot(hot, lab_low[...]).astype(BF16)

    inverse_load.wait()

    @pl.loop(0, tiles)
    def _(step):
        rows = rows_of(step)
        value = dot3(split(inverse[rows, :]), (rhs_high[...], rhs_low[...]))
        sol_h[rows, :], sol_l[rows, :] = split(value)

    @pl.when(inner)
    def _():
        two_from.wait_recv()
        two_pass.start()

    proj_all[r] = dot3(split(basis[...].T), (sol_h[...], sol_l[...]))

    @pl.when(outer)
    def _():
        proj_end.start()

    @pl.when(inner)
    def _():
        proj_over.start()

    basis_parts = split(basis[...])
    lab_high[:, :rank], lab_low[:, :rank] = basis_parts

    @pl.loop(0, tiles)
    def _(step):
        rows = rows_of(step)
        value = dot3(split(inverse[rows, :]), (lab_high[:, :rank], lab_low[:, :rank]))
        rhs_high[rows, :rank], rhs_low[rows, :rank] = split(value)

    @pl.when(outer)
    def _():
        proj_end.wait_send()
        for c in couple_end[1:]:
            c.start()

    @pl.when(inner)
    def _():
        two_over.wait_recv()
        two_across.start()
        proj_from.wait_recv()
        proj_pass.start()

    def hot_rows(step):
        hot = (lax.broadcasted_iota(jnp.int32, (tile, leaf), 0) + step * tile) == order[...]
        return hot.astype(F32).astype(BF16)

    @pl.loop(0, tiles)
    def _(step):
        rows = rows_of(step)
        hot = hot_rows(step)
        placed_out[rows, :] = dot(hot, sol_h[...]) + dot(hot, sol_l[...])

    placed_store = pltpu.make_async_copy(placed_out, placed_hbm, local_sem.at[1])
    placed_store.start()

    for c in tops:
        c.wait_recv()
    row_top = [over_row(0, top_rows.at[q, r], top_rows.at[q, r], s) for s in range(1, FAN)]
    for c in row_top:
        c.start()

    @pl.when(inner)
    def _():
        two_pass.wait_recv()
        two_beyond.start()
        proj_over.wait_recv()
        proj_pass.wait_recv()

    @pl.when(outer)
    def _():
        two_own.wait_recv()
        two_across.wait_recv()
        two_beyond.wait_recv()

    trans_two_all[q] = couple_two_all[:, :, width:]
    quad_two = [
        over_quad(0, trans_two_all.at[q], trans_two_all.at[q], s) for s in range(1, FAN)
    ]
    for c in quad_two:
        c.start()

    for c in row_top:
        c.wait_recv()
    quad_top = [over_quad(3, top_rows.at[q], top_rows.at[q], s) for s in range(1, FAN)]
    for c in quad_top:
        c.start()

    @pl.when(inner)
    def _():
        own_couple = split(couple_one[...])
        own_trans = split(transfer_one[...].T)
        for c in couple_end:
            c.wait_recv()
        trans_from.wait_recv()
        ward_couple = split(couple_ward[...])
        ward_trans = split(trans_one_all[mate].T)

        def level_one(pair):
            here = pl.ds(pl.multiple_of(pair * 2 * part_cols, 2 * part_cols), 2 * part_cols)
            stack_one = split(flat(proj_all[:, :, here]))
            own = dot3(own_couple, stack_one)
            ward = dot3(ward_couple, stack_one)
            solve_one[:, here] = own
            solve_ward[:, here] = ward
            reduced = dot3(own_trans, split(own)) + dot3(ward_trans, split(ward))
            for part in range(2):
                reduce_part[pair * 2 + part] = reduced[
                    :, part * part_cols : (part + 1) * part_cols
                ]

        level_one(1 - r // 2)
        reduce_over.start()
        level_one(r // 2)
        reduce_over.wait_recv()
        ward_part[...] = reduce_part[mate] + reduce_in[mate % 2]
        reduce_ward.start()
        stack_two[q] = reduce_part[r] + reduce_in[r % 2]

    @pl.when(outer)
    def _():
        reduce_ward.wait_recv()

    beside = q + 1 - 2 * (q % 2)
    opposite = (q + 2) % FAN

    def stack_copy(slot, to, number):
        return copy(
            stack_two.at[slot], stack_two.at[slot], quad_send.at[1, number],
            quad_recv.at[1, number], device(g * FAN + to, r),
        )

    quad_stack = [
        stack_copy(q, opposite, 0), stack_copy(q, beside, 1), stack_copy(opposite, beside, 2)
    ]
    quad_stack[0].start()
    quad_stack[1].start()

    @pl.when(inner)
    def _():
        trans_pass.start()
        solve_back.start()

    @pl.loop(0, tiles)
    def _(step):
        rows = rows_of(step)
        hot = hot_rows(step)
        spread_high[rows, :] = dot(hot, rhs_high[:, :rank]).astype(BF16)
        spread_low[rows, :] = dot(hot, rhs_low[:, :rank]).astype(BF16)

    spread_store = [
        pltpu.make_async_copy(spread_high, spread_high_hbm, local_sem.at[2]),
        pltpu.make_async_copy(spread_low, spread_low_hbm, local_sem.at[3]),
    ]
    for c in spread_store:
        c.start()


    quad_stack[0].wait_recv()
    quad_stack[2].start()
    couple = split(flat(couple_two_all[:, :, :width]))
    for c in quad_two:
        c.wait_recv()
    gain_two = split(dot3(couple, split(flat(trans_two_all[...]))))
    own_two = flat(trans_two_all[q]).T
    for c in quad_stack[1:]:
        c.wait_recv()
    solve_two = dot3(couple, split(flat(stack_two[...])))
    top_part[...] = matmul(own_two, solve_two).reshape(FAN, part_rows, part_cols)
    quad_reduce = [
        over_quad(2, top_part.at[(q + s) % FAN], top_in.at[s - 1], s) for s in range(1, FAN)
    ]
    for c in quad_reduce:
        c.start()
    for c in quad_reduce:
        c.wait_recv()
    top_all[sid] = top_part[q] + top_in[0] + (top_in[1] + top_in[2])
    wide_top = [over_wide(top_all.at[sid], top_all.at[sid], s) for s in range(1, wide)]
    for c in wide_top:
        c.start()
    for c in wide_top:
        c.wait_recv()
    for c in quad_top:
        c.wait_recv()
    total = jnp.zeros((rank, part_cols), F32)
    for other in range(groups):
        total = total + matmul(
            flat(top_rows[:, :, other]), flat(top_all[other * FAN : (other + 1) * FAN])
        )
    fixed_two_all[r] = solve_two - dot3(gain_two, split(total))
    line_start(fixed_two_all, 0, 0)

    @pl.when(inner)
    def _():
        trans_over.wait_recv()
        trans_pass.wait_recv()
        trans_full = split(flat(trans_one_all[...]))
        gain_ward[...] = dot3(split(couple_ward[...]), trans_full)
        gain_back.start()
        gain_one[...] = dot3(split(couple_one[...]), trans_full)

    line_wait(fixed_two_all, 0, 0)
    line_start(fixed_two_all, 0, 1)
    line_wait(fixed_two_all, 0, 1)
    line_start(fixed_two_all, 0, 2)
    line_wait(fixed_two_all, 0, 2)

    @pl.when(outer)
    def _():
        solve_back.wait_recv()
        gain_back.wait_recv()

    gain = split(gain_one[...])
    for part in range(FAN):
        here = slice(part * part_cols, (part + 1) * part_cols)
        value = solve_one[:, here] - dot3(gain, split(fixed_two_all[part]))
        block_high[:, here], block_low[:, here] = split(value)

    for which, buf in enumerate((fixed_two_all,)):
        line_finish(buf, which)

    @pl.when(outer)
    def _():
        for c in couple_end:
            c.wait_send()
        trans_end.wait_send()
        two_end.wait_send()

    @pl.when(inner)
    def _():
        for c in (
            proj_over, proj_pass, trans_over, trans_pass, reduce_over, reduce_ward,
            solve_back, gain_back, two_over, two_pass, two_own, two_across, two_beyond,
        ):
            c.wait_send()

    for c in tops + row_top + quad_two + quad_stack + quad_reduce + wide_top + quad_top:
        c.wait_send()
    placed_store.wait()
    for c in spread_store:
        c.wait()


def last(placed, spread_high, spread_low, block_high, block_low, out):
    out[...] = placed[...] - dot3(
        (spread_high[...], spread_low[...]), (block_high[...], block_low[...])
    )


def per_device(
    depth,
    groups,
    labels,
    point_order,
    leaf_inverse,
    leaf_basis,
    couple_one,
    transfer_one,
    couple_two,
    transfer_two,
    couple_top,
):
    leaf, cols = labels.shape
    rank = leaf_basis.shape[1]
    part_cols = cols // FAN
    part_rows = rank // FAN
    slice_rows = couple_top.shape[0] // groups
    wide = FAN * groups
    vmem = pl.BlockSpec(memory_space=pltpu.VMEM)
    far = pl.BlockSpec(memory_space=pl.ANY)
    dma = pltpu.SemaphoreType.DMA
    args = (
        labels, point_order, leaf_inverse, leaf_basis, couple_one, transfer_one,
        couple_two, transfer_two, couple_top,
    )
    placed, *parts = pl.pallas_call(
        functools.partial(kernel, depth, groups, leaf // TILES),
        out_shape=(
            jax.ShapeDtypeStruct((leaf, cols), F32),
            jax.ShapeDtypeStruct((leaf, rank), BF16),
            jax.ShapeDtypeStruct((leaf, rank), BF16),
            jax.ShapeDtypeStruct((rank, cols), BF16),
            jax.ShapeDtypeStruct((rank, cols), BF16),
        ),
        in_specs=[vmem, vmem, far] + [vmem] * (len(args) - 3),
        out_specs=(far, far, far, vmem, vmem),
        scratch_shapes=[
            pltpu.VMEM((leaf, cols), F32),
            pltpu.VMEM((leaf, rank), BF16),
            pltpu.VMEM((leaf, rank), BF16),
            pltpu.VMEM((leaf, leaf), F32),
            pltpu.VMEM((leaf, cols), BF16),
            pltpu.VMEM((leaf, cols), BF16),
            pltpu.VMEM((2, leaf, cols), BF16),
            pltpu.VMEM((2, leaf, cols), BF16),
            pltpu.VMEM((leaf, 128), jnp.int32),
            pltpu.VMEM((FAN, rank, cols), F32),
            pltpu.VMEM((FAN, *transfer_one.shape), F32),
            pltpu.VMEM((FAN, couple_two.shape[0], couple_two.shape[1] + rank), F32),
            pltpu.VMEM((FAN, rank, part_cols), F32),
            pltpu.VMEM((FAN, rank, part_cols), F32),
            pltpu.VMEM((2, rank, part_cols), F32),
            pltpu.VMEM((FAN, rank, part_cols), F32),
            pltpu.VMEM((FAN, FAN, *transfer_two.shape), F32),
            pltpu.VMEM((FAN, part_rows, part_cols), F32),
            pltpu.VMEM((FAN - 1, part_rows, part_cols), F32),
            pltpu.VMEM((wide, part_rows, part_cols), F32),
            pltpu.VMEM((FAN, FAN, groups, slice_rows, rank), F32),
            pltpu.VMEM((rank, cols), F32),
            pltpu.VMEM((rank, rank), F32),
            pltpu.VMEM(couple_one.shape, F32),
            pltpu.VMEM((rank, cols), F32),
            pltpu.VMEM((rank, rank), F32),
            pltpu.VMEM((rank, part_cols), F32),
            dma((20,)),
            dma((20,)),
            dma((4,)),
            dma((1, 2, FAN - 1)),
            dma((1, 2, FAN - 1)),
            dma((1, FAN - 1)),
            dma((1, FAN - 1)),
            dma((4, FAN - 1)),
            dma((4, FAN - 1)),
            dma((wide - 1,)),
            dma((wide - 1,)),
            dma((max(groups - 1, 1),)),
            dma((max(groups - 1, 1),)),
        ],
        compiler_params=pltpu.CompilerParams(
            collective_id=0, has_side_effects=True, vmem_limit_bytes=56 * 1024 * 1024
        ),
    )(*args)
    tile = leaf // 4
    spread_spec = pl.BlockSpec((tile, rank), lambda i: (i, 0))
    block_spec = pl.BlockSpec((rank, cols), lambda i: (0, 0))
    return pl.pallas_call(
        last,
        out_shape=jax.ShapeDtypeStruct((leaf, cols), F32),
        grid=(leaf // tile,),
        in_specs=[
            pl.BlockSpec((tile, cols), lambda i: (i, 0)),
            spread_spec, spread_spec, block_spec, block_spec,
        ],
        out_specs=pl.BlockSpec((tile, cols), lambda i: (i, 0)),
        compiler_params=pltpu.CompilerParams(vmem_limit_bytes=60 * 1024 * 1024),
    )(placed, *parts)


def solution(mesh):
    depth = mesh.shape["gy"]
    groups = mesh.shape["gx"] * depth // (FAN * FAN)
    spec = P(("gx", "gy"), None)
    return jax.shard_map(
        functools.partial(per_device, depth, groups),
        mesh=mesh,
        in_specs=(spec,) * 9,
        out_specs=spec,
        check_vma=False,
    )
```
